32 devices in a mesh: ang: 16 (over z, y, core), dist: 2 (over x).
Axes of the slice: x: 2, y: 2, z: 4, core: 2. Of those that a mesh axis runs over, the one named last changes fastest.
Arguments:
- volume: float32 [16, 1024, 1024], P('ang', 'dist'), may hold values from -0.2 to 0.2
- row_weights: float32 [64, 1024], replicated, may hold values from 0.2 to 2
- angle_slope: int32 [64], replicated, may hold values from -1024 to 1023, as said below
- shear_index: int32 [64, 1024], replicated, may hold values from 0 to 1022, as said below
- shear_weight: float32 [64, 1024], replicated, as said below
- fresnel: float32 [2], P('dist'), may hold values from 20 to 80
- measured: float32 [2, 64, 16, 1024], P('dist', 'ang'), may hold values from 0.3 to 1.7
Outputs:
- volume_grad: float32 [16, 1024, 1024], P('ang', 'dist')
The draws below stay inside these ranges and needn't reach their ends.
Inputs may be any that keep to these rules, and one draw needn't show every extreme that they name: `angle_slope`: distinct values, one in each of 64 equal runs of the range, in an order drawn from the seed. shear_index[a, u] = floor(P[a, u] / 4096) + 512 with P[a, u] = (3072 + angle_slope[a]) * (u - 512). shear_weight[a, u] = (P[a, u] mod 4096) / 4096 with the same P.
All inputs are finite; a program needn't handle non-finite values.
Results may differ from the reference program's by a relative error of at most 0.0003.
Values sent between devices are 32-bit elements; how exact they have to be, the bound alone decides.
A program may use at most 64 MiB of HBM per device.

```python
import math
import jax
import jax.numpy as jnp
from jax import lax

N = 1024
SLICES = 16
ANGLES = 64
DISTS = 2


def slope_list(key):
    step_size = 2048 // ANGLES
    jitter = jax.random.randint(jax.random.fold_in(key, 101), (ANGLES,), 0, step_size)
    counter = jnp.arange(ANGLES, dtype=jnp.int32)
    jitter = jnp.where(counter == 0, 0, jnp.where(counter == ANGLES - 1, step_size - 1, jitter))
    values = counter * step_size - 1024 + jitter
    shuffle = jax.random.permutation(jax.random.fold_in(key, 102), ANGLES)
    return values[shuffle].astype(jnp.int32)


def shear_product(key):
    slopes = slope_list(key)
    column = jnp.arange(N, dtype=jnp.int32) - N // 2
    return (3072 + slopes)[:, None] * column[None, :]


def draw_angle_slope(key, part):
    shared = slope_list(key)
    return shared


def draw_shear_index(key, part):
    product = shear_product(key)
    return (jnp.floor_divide(product, 4096) + N // 2).astype(jnp.int32)


def draw_shear_weight(key, part):
    product = shear_product(key)
    return jnp.remainder(product, 4096).astype(jnp.float32) / 4096.0


def block_scale(stream_key, shape, cuts, least, top_value):
    factor_of = 1.0
    for axis_at, blocks in cuts:
        heights = jax.random.uniform(jax.random.fold_in(jax.random.fold_in(stream_key, 6), axis_at), (blocks,), jnp.float32, least / len(cuts), top_value / len(cuts))
        factor_of = factor_of * jnp.repeat(jnp.exp(heights), shape[axis_at] // blocks).reshape((-1,) + (1,) * (len(shape) - 1 - axis_at))
    return factor_of


def noise(stream_key, dims, deviation, reach, split=(), held_as=jnp.bfloat16):
    loudness = block_scale(stream_key, dims, split, -0.22, 0.18) if split else 1.0
    result = jax.random.normal(stream_key, dims, jnp.float32) * deviation * loudness
    return jnp.minimum(jnp.maximum(result, -reach), reach).astype(held_as)


def setup_inputs(seed: int = 0) -> dict:
    seeds = jax.random.split(jax.random.key(seed), 8)
    return {
        "volume": noise(seeds[0], (SLICES, N, N), 0.03, 0.2, ((0, 16), (1, 2)), jnp.float32),
        "row_weights": jnp.clip(jnp.exp(jax.random.uniform(seeds[1], (ANGLES, N), jnp.float32, math.log(0.2), math.log(2.0))), 0.2, 2.0),
        "angle_slope": draw_angle_slope(jax.random.fold_in(seeds[7], 71), 0),
        "shear_index": draw_shear_index(jax.random.fold_in(seeds[7], 71), 0),
        "shear_weight": draw_shear_weight(jax.random.fold_in(seeds[7], 71), 0),
        "fresnel": jnp.clip(jnp.exp(math.log(80.0) - 1.3862944 * jax.random.uniform(seeds[5], (DISTS,), jnp.float32) ** block_scale(seeds[5], (DISTS,), ((0, 2),), -0.2, 0.2)), 20.0, 80.0),
        "measured": jnp.clip(0.3 + 1.40000004 * jax.random.uniform(seeds[6], (DISTS, ANGLES, SLICES, N), jnp.float32) ** block_scale(seeds[6], (DISTS, ANGLES, SLICES, N), ((0, 2), (1, 16)), -0.2, 0.2), 0.3, 1.7),
    }


ABSORB = 0.1

def frequencies(length, float_type):
    counter = jnp.arange(length, dtype=jnp.int32)
    signed = jnp.where(counter <= (length - 1) // 2, counter, counter - length)
    return signed.astype(float_type) / length

def resample(rays, shear_index, shear_weight, path_scale):
    lower_index = jnp.broadcast_to(shear_index[:, None, :], rays.shape)
    lower_tap = jnp.take_along_axis(rays, lower_index, axis=2)
    upper_tap = jnp.take_along_axis(rays, lower_index + 1, axis=2)
    weight_col = shear_weight[:, None, :]
    return path_scale[:, None, None] * ((1.0 - weight_col) * lower_tap + weight_col * upper_tap)

def reference(volume, row_weights, angle_slope, shear_index, shear_weight, fresnel, measured):
    path_scale = jnp.sqrt(1.0 + (angle_slope.astype(jnp.float32) / 512.0) ** 2)

    def objective(volume_in):
        rays = jnp.einsum('ay,zyx->azx', row_weights, volume_in, precision=lax.Precision.HIGHEST)
        projected = resample(rays, shear_index, shear_weight, path_scale)
        attenuation = jnp.exp(-ABSORB * projected)
        wavefield = attenuation * jnp.cos(projected) + 1j * (attenuation * jnp.sin(projected))
        spectrum = jnp.fft.fft2(wavefield)
        freq_rows = frequencies(SLICES, volume_in.dtype)
        freq_cols = frequencies(N, volume_in.dtype)
        loss_sum = jnp.zeros((), volume_in.dtype)
        for distance in range(DISTS):
            phase_table = jnp.pi * fresnel[distance] * (freq_rows[:, None] ** 2 + freq_cols[None, :] ** 2)
            propagator = jnp.cos(phase_table) - 1j * jnp.sin(phase_table)
            detector_field = jnp.fft.ifft2(spectrum * propagator)
            intensity = jnp.real(detector_field) ** 2 + jnp.imag(detector_field) ** 2
            loss_sum = loss_sum + jnp.sum((intensity - measured[distance]) ** 2)
        return loss_sum / ANGLES
    return jax.grad(objective)(volume)
```

```python
from functools import partial
import math

import numpy as np
import jax
import jax.numpy as jnp
from jax import lax
from jax.experimental import pallas as pl
from jax.experimental.pallas import tpu as pltpu
from jax.sharding import PartitionSpec as P

ABSORB = 0.1
HIGHEST = lax.Precision.HIGHEST
LANES = 128


def dot(a, b):
    return lax.dot_general(
        a, b, (((1,), (0,)), ((), ())), precision=HIGHEST, preferred_element_type=jnp.float32
    )


def signed_freq(counter, length):
    return np.where(counter <= (length - 1) // 2, counter, counter - length) / length


def column_tables(width):
    outer = width // LANES
    p = np.arange(LANES)
    k = np.arange(outer)
    ang = 2 * np.pi * (p[:, None] * p[None, :] % LANES) / LANES
    c, s = np.cos(ang), np.sin(ang)
    forward = np.block([[c, -s], [s, c]])
    inverse = np.block([[c, s], [-s, c]])
    mixed = 2 * np.pi * (k[:, None] * p[None, :] % width) / width
    freq2 = signed_freq(k[:, None] + outer * p[None, :], width) ** 2
    small = np.stack([np.cos(mixed), np.sin(mixed), freq2])
    return forward.astype(np.float32), inverse.astype(np.float32), small.astype(np.float32)


def row_tables(slices, angles):
    z = np.arange(slices)
    ang = 2 * np.pi * (z[:, None] * z[None, :] % slices) / slices
    trig = np.stack([np.cos(ang), np.sin(ang)])
    rows = 2 * angles * slices
    left_r = np.zeros((2, angles, slices, 2, angles, 2, slices))
    left_i = np.zeros_like(left_r)
    right = np.zeros((2, angles, 2, slices, 2, angles, slices))
    for c in range(2):
        for a in range(angles):
            for t in range(2):
                left_r[c, a, :, c, a, t, :] = trig[t]
                left_i[c, a, :, 1 - c, a, t, :] = trig[t] * (-1.0 if c == 0 else 1.0)
                right[c, a, t, :, c, a, :] = trig[t] / slices
    freq2 = np.broadcast_to(signed_freq(z, slices) ** 2, (2, angles, 2, slices)).reshape(1, -1)
    left = np.stack([left_r.reshape(rows, -1), left_i.reshape(rows, -1)])
    return left.astype(np.float32), right.reshape(-1, rows).astype(np.float32), freq2.astype(np.float32)


def fft_list(parts, sign):
    n = len(parts)
    if n == 1:
        return parts
    even = fft_list(parts[0::2], sign)
    odd = fft_list(parts[1::2], sign)
    low, high = [], []
    for k in range(n // 2):
        (er, ei), (br, bi) = even[k], odd[k]
        if k == 0:
            tr, ti = br, bi
        elif 4 * k == n:
            tr, ti = (-bi, br) if sign > 0 else (bi, -br)
        else:
            wr = math.cos(2 * math.pi * k / n)
            wi = sign * math.sin(2 * math.pi * k / n)
            tr, ti = br * wr - bi * wi, br * wi + bi * wr
        low.append((er + tr, ei + ti))
        high.append((er - tr, ei - ti))
    return low + high


def columns_forward(parts, table, mix_cos, mix_sin):
    parts = fft_list(parts, -1)
    rows = []
    for k, (re, im) in enumerate(parts):
        c, s = mix_cos[k : k + 1], mix_sin[k : k + 1]
        rows.append(jnp.concatenate([re * c + im * s, im * c - re * s], axis=1))
    return dot(jnp.concatenate(rows, axis=0), table)


def columns_inverse(spectrum, table, mix_cos, mix_sin):
    outer = mix_cos.shape[0]
    count = spectrum.shape[0] // outer
    result = dot(spectrum, table)
    parts = []
    for k in range(outer):
        re = result[k * count : (k + 1) * count, :LANES]
        im = result[k * count : (k + 1) * count, LANES:]
        c, s = mix_cos[k : k + 1], mix_sin[k : k + 1]
        parts.append((re * c - im * s, im * c + re * s))
    return fft_list(parts, 1)


def tile_pairs(outer):
    pairs = []
    half = outer // 2
    for block in range(outer):
        first = LANES * (block - half)
        ends = [first, first + LANES - 1]
        low = min(min(math.floor(u * 0.5), math.floor(u * 4095 / 4096)) for u in ends)
        high = max(max(math.floor(u * 0.5), math.floor(u * 4095 / 4096)) for u in ends) + 1
        for tile in range(low // LANES + half, high // LANES + half + 1):
            if 0 <= tile < outer:
                pairs.append((block, tile))
    return pairs


def lane_take(values, index):
    return jnp.take_along_axis(values, index, axis=1, mode="promise_in_bounds")


def band_forward(tiles, step):
    outer, count = len(tiles), tiles[0].shape[0]
    lane = lax.broadcasted_iota(jnp.int32, (1, LANES), 1).astype(jnp.float32)
    center = float(outer // 2 * LANES)
    result = [None] * outer
    for block in range(outer):
        place = step * (lane + (LANES * block - center)) * (1.0 / 4096.0)
        lower = jnp.floor(place)
        weight = place - lower
        for shift, coef in ((0.0, 1.0 - weight), (1.0, weight)):
            source = lower + (center + shift)
            tile_of = jnp.floor(source * (1.0 / LANES))
            inside = (source - LANES * tile_of).astype(jnp.int32)
            index = jnp.broadcast_to(inside, (count, LANES))
            for pair_block, tile in tile_pairs(outer):
                if pair_block != block:
                    continue
                term = jnp.where(tile_of == float(tile), coef, 0.0) * lane_take(tiles[tile], index)
                result[block] = term if result[block] is None else result[block] + term
    return result


def band_backward(blocks, step):
    outer, count = len(blocks), blocks[0].shape[0]
    lane = lax.broadcasted_iota(jnp.int32, (1, LANES), 1).astype(jnp.float32)
    center = float(outer // 2 * LANES)
    result = [None] * outer
    for tile in range(outer):
        target = (lane + (LANES * tile - center)) * 4096.0
        first = jnp.floor(target / step)
        for shift in (-1.0, 0.0, 1.0, 2.0):
            source = first + shift
            coef = jnp.maximum(4096.0 - jnp.abs(step * source - target), 0.0) * (1.0 / 4096.0)
            place = source + center
            block_of = jnp.floor(place * (1.0 / LANES))
            inside = (place - LANES * block_of).astype(jnp.int32)
            index = jnp.broadcast_to(inside, (count, LANES))
            for block, pair_tile in tile_pairs(outer):
                if pair_tile != tile:
                    continue
                term = jnp.where(block_of == float(block), coef, 0.0) * lane_take(blocks[block], index)
                result[tile] = term if result[tile] is None else result[tile] + term
    return result


def image_step(ray_tiles, slopes, fresnels, measured, tables, angles_total):
    forward, inverse, small, left, right, row_freq2 = tables
    angles, outer = len(ray_tiles), len(ray_tiles[0])
    slices = ray_tiles[0][0].shape[0]
    rows = angles * slices
    width = outer * LANES
    mix_cos, mix_sin, col_freq2 = small
    scales, steps = [], []
    for slope in slopes:
        value = slope.astype(jnp.float32)
        steps.append(value + 3072.0)
        tangent = jnp.full((1, LANES), value) * (1.0 / 512.0)
        scales.append(jnp.sqrt(1.0 + tangent * tangent))
    images = [band_forward(ray_tiles[a], steps[a]) for a in range(angles)]
    waves = []
    for q in range(outer):
        image = jnp.concatenate([images[a][q] * scales[a] for a in range(angles)], axis=0)
        fade = jnp.exp(-ABSORB * image)
        waves.append((fade * jnp.cos(image), fade * jnp.sin(image)))
    spectrum = columns_forward(waves, forward, mix_cos, mix_sin)
    spec_re = [spectrum[k * rows : (k + 1) * rows, :LANES] for k in range(outer)]
    spec_im = [spectrum[k * rows : (k + 1) * rows, LANES:] for k in range(outer)]
    total = [None] * outer
    for d in range(len(fresnels)):
        phase = (math.pi * fresnels[d]) * col_freq2
        col_cos, col_sin = jnp.cos(phase), jnp.sin(phase)
        row_phase = (math.pi * fresnels[d]) * row_freq2
        left_cos, left_sin = left[0] * jnp.cos(row_phase), left[1] * jnp.sin(row_phase)
        mix = dot(left_cos - left_sin, right)
        mix_back = dot(left_cos + left_sin, right)
        scaled = []
        for k in range(outer):
            c, s = col_cos[k : k + 1], col_sin[k : k + 1]
            re, im = spec_re[k], spec_im[k]
            scaled.append(jnp.concatenate([re * c + im * s, im * c - re * s], axis=1))
        parts = columns_inverse(jnp.concatenate(scaled, axis=0), inverse, mix_cos, mix_sin)
        stacked = jnp.concatenate([jnp.concatenate(part, axis=0) for part in parts], axis=1)
        field = dot(mix, stacked * (1.0 / width))
        re, im = field[:rows], field[rows:]
        slope_of = (re * re + im * im - measured[d]) * (4.0 / angles_total)
        back = dot(mix_back, jnp.concatenate([slope_of * re, slope_of * im], axis=0))
        pieces = [
            (back[:rows, q * LANES : (q + 1) * LANES], back[rows:, q * LANES : (q + 1) * LANES])
            for q in range(outer)
        ]
        adjoint = columns_forward(pieces, forward, mix_cos, mix_sin)
        for k in range(outer):
            c, s = col_cos[k : k + 1], col_sin[k : k + 1]
            re = adjoint[k * rows : (k + 1) * rows, :LANES]
            im = adjoint[k * rows : (k + 1) * rows, LANES:]
            term = jnp.concatenate([re * c - im * s, im * c + re * s], axis=1)
            total[k] = term if total[k] is None else total[k] + term
    parts = columns_inverse(jnp.concatenate(total, axis=0), inverse, mix_cos, mix_sin)
    grads = []
    for q in range(outer):
        (re, im), (wave_re, wave_im) = parts[q], waves[q]
        re, im = re * (1.0 / width), im * (1.0 / width)
        grads.append(re * (-ABSORB * wave_re - wave_im) + im * (wave_re - ABSORB * wave_im))
    result = []
    for a in range(angles):
        own = [g[a * slices : (a + 1) * slices] * scales[a] for g in grads]
        result.append(band_backward(own, steps[a]))
    return result


def image_kernel(
    angles, slices, outer, angles_total,
    slope_ref, fresnel_ref, other_fresnel_ref, own_ref, other_ref, ray_ref,
    forward_ref, inverse_ref, small_ref, left_ref, right_ref, freq_ref, out_ref,
):
    stride = 2 * angles * outer
    rays = []
    for a in range(angles):
        rays.append([
            ray_ref[pl.ds(a * outer + q, slices, stride), :]
            + ray_ref[pl.ds((angles + a) * outer + q, slices, stride), :]
            for q in range(outer)
        ])
    rows = angles * slices
    tables = (
        forward_ref[...], inverse_ref[...], (small_ref[0], small_ref[1], small_ref[2]),
        (left_ref[0], left_ref[1]), right_ref[...], freq_ref[...],
    )
    result = image_step(
        rays, [slope_ref[a] for a in range(angles)], [fresnel_ref[0], other_fresnel_ref[0]],
        [own_ref[...].reshape(rows, outer * LANES), other_ref[...].reshape(rows, outer * LANES)],
        tables, angles_total,
    )
    for a in range(angles):
        for q in range(outer):
            for copy in range(2):
                out_ref[pl.ds((copy * angles + a) * outer + q, slices, stride), :] = result[a][q]


def image_call(slopes, fresnel, other_fresnel, own, other, rays, angles_total):
    angles, slices, width = own.shape
    outer = width // LANES
    tables = column_tables(width) + row_tables(slices, angles)
    smem = pl.BlockSpec(memory_space=pltpu.SMEM)
    vmem = pl.BlockSpec(memory_space=pltpu.VMEM)
    return pl.pallas_call(
        partial(image_kernel, angles, slices, outer, angles_total),
        out_shape=jax.ShapeDtypeStruct(rays.shape, jnp.float32),
        in_specs=[smem] * 3 + [vmem] * 9,
        out_specs=vmem,
        compiler_params=pltpu.CompilerParams(vmem_limit_bytes=48 * 2**20),
    )(slopes, fresnel, other_fresnel, own, other, rays, *[jnp.asarray(t) for t in tables])


def shards(volume, row_weights, angle_slope, shear_index, shear_weight, fresnel, measured):
    row_count, width = volume.shape[1], volume.shape[2]
    angles_total = row_weights.shape[0]
    group, slices = measured.shape[1], measured.shape[2]
    angles = group // 2
    outer = width // LANES
    both = ("ang", "dist")
    dist = lax.axis_index("dist")
    mine = (lax.axis_index("ang") * 2 + dist) * angles
    swap = [(0, 1), (1, 0)]
    own = lax.dynamic_slice_in_dim(measured[0], dist * angles, angles, 0)
    other = lax.ppermute(
        lax.dynamic_slice_in_dim(measured[0], (1 - dist) * angles, angles, 0), "dist", swap
    )
    other_fresnel = lax.ppermute(fresnel, "dist", swap)
    slopes = lax.dynamic_slice_in_dim(angle_slope, mine, angles, 0)
    own_weights = lax.dynamic_slice_in_dim(row_weights, dist * row_count, row_count, 1)
    rays = jnp.einsum("ay,yx->ax", own_weights, volume[0], precision=HIGHEST)
    rays = lax.all_to_all(rays.reshape(angles_total, outer, LANES), both, 0, 0, tiled=True)
    spread = image_call(
        slopes, fresnel, other_fresnel, own, other, rays.reshape(-1, LANES), angles_total
    )
    spread = lax.all_to_all(spread.reshape(angles_total, outer, LANES), both, 0, 0, tiled=True)
    spread = spread.reshape(angles_total, width)
    return jnp.einsum("ay,ax->yx", own_weights, spread, precision=HIGHEST)[None]


def solution(mesh):
    placed = (P("ang", "dist", None), P(), P(), P(), P(), P("dist"), P("dist", "ang", None, None))
    return jax.shard_map(
        shards, mesh=mesh, in_specs=placed, out_specs=P("ang", "dist", None), check_vma=False
    )
```

```python
from functools import partial
import math

import numpy as np
import jax
import jax.numpy as jnp
from jax import lax
from jax.experimental import pallas as pl
from jax.experimental.pallas import tpu as pltpu
from jax.sharding import PartitionSpec as P

ABSORB = 0.1
HIGHEST = lax.Precision.HIGHEST
LANES = 128


def dot(a, b):
    return lax.dot_general(
        a, b, (((1,), (0,)), ((), ())), precision=HIGHEST, preferred_element_type=jnp.float32
    )


def signed_freq(counter, length):
    return np.where(counter <= (length - 1) // 2, counter, counter - length) / length


def column_tables(width):
    outer = width // LANES
    p = np.arange(LANES)
    k = np.arange(outer)
    ang = 2 * np.pi * (p[:, None] * p[None, :] % LANES) / LANES
    c, s = np.cos(ang), np.sin(ang)
    forward = np.block([[c, -s], [s, c]])
    inverse = np.block([[c, s], [-s, c]])
    mixed = 2 * np.pi * (k[:, None] * p[None, :] % width) / width
    freq2 = signed_freq(k[:, None] + outer * p[None, :], width) ** 2
    small = np.stack([np.cos(mixed), np.sin(mixed), freq2])
    return forward.astype(np.float32), inverse.astype(np.float32), small.astype(np.float32)


def row_tables(slices, angles):
    z = np.arange(slices)
    ang = 2 * np.pi * (z[:, None] * z[None, :] % slices) / slices
    trig = np.stack([np.cos(ang), np.sin(ang)])
    rows = 2 * angles * slices
    left_r = np.zeros((2, angles, slices, 2, angles, 2, slices))
    left_i = np.zeros_like(left_r)
    right = np.zeros((2, angles, 2, slices, 2, angles, slices))
    for c in range(2):
        for a in range(angles):
            for t in range(2):
                left_r[c, a, :, c, a, t, :] = trig[t]
                left_i[c, a, :, 1 - c, a, t, :] = trig[t] * (-1.0 if c == 0 else 1.0)
                right[c, a, t, :, c, a, :] = trig[t] / slices
    freq2 = np.broadcast_to(signed_freq(z, slices) ** 2, (2, angles, 2, slices)).reshape(1, -1)
    left = np.stack([left_r.reshape(rows, -1), left_i.reshape(rows, -1)])
    return left.astype(np.float32), right.reshape(-1, rows).astype(np.float32), freq2.astype(np.float32)


def fft_list(parts, sign):
    n = len(parts)
    if n == 1:
        return parts
    even = fft_list(parts[0::2], sign)
    odd = fft_list(parts[1::2], sign)
    low, high = [], []
    for k in range(n // 2):
        (er, ei), (br, bi) = even[k], odd[k]
        if k == 0:
            tr, ti = br, bi
        elif 4 * k == n:
            tr, ti = (-bi, br) if sign > 0 else (bi, -br)
        else:
            wr = math.cos(2 * math.pi * k / n)
            wi = sign * math.sin(2 * math.pi * k / n)
            tr, ti = br * wr - bi * wi, br * wi + bi * wr
        low.append((er + tr, ei + ti))
        high.append((er - tr, ei - ti))
    return low + high


def columns_forward(parts, table, mix_cos, mix_sin):
    parts = fft_list(parts, -1)
    rows = []
    for k, (re, im) in enumerate(parts):
        c, s = mix_cos[k : k + 1], mix_sin[k : k + 1]
        rows.append(jnp.concatenate([re * c + im * s, im * c - re * s], axis=1))
    return dot(jnp.concatenate(rows, axis=0), table)


def columns_inverse(spectrum, table, mix_cos, mix_sin):
    outer = mix_cos.shape[0]
    count = spectrum.shape[0] // outer
    result = dot(spectrum, table)
    parts = []
    for k in range(outer):
        re = result[k * count : (k + 1) * count, :LANES]
        im = result[k * count : (k + 1) * count, LANES:]
        c, s = mix_cos[k : k + 1], mix_sin[k : k + 1]
        parts.append((re * c - im * s, im * c + re * s))
    return fft_list(parts, 1)


def tile_pairs(outer):
    pairs = []
    half = outer // 2
    for block in range(outer):
        first = LANES * (block - half)
        ends = [first, first + LANES - 1]
        low = min(min(math.floor(u * 0.5), math.floor(u * 4095 / 4096)) for u in ends)
        high = max(max(math.floor(u * 0.5), math.floor(u * 4095 / 4096)) for u in ends) + 1
        for tile in range(low // LANES + half, high // LANES + half + 1):
            if 0 <= tile < outer:
                pairs.append((block, tile))
    return pairs


def lane_take(values, index):
    return jnp.take_along_axis(values, index, axis=1, mode="promise_in_bounds")


def band_forward(tiles, step):
    outer, count = len(tiles), tiles[0].shape[0]
    lane = lax.broadcasted_iota(jnp.int32, (1, LANES), 1).astype(jnp.float32)
    center = float(outer // 2 * LANES)
    result = [None] * outer
    for block in range(outer):
        place = step * (lane + (LANES * block - center)) * (1.0 / 4096.0)
        lower = jnp.floor(place)
        weight = place - lower
        for shift, coef in ((0.0, 1.0 - weight), (1.0, weight)):
            source = lower + (center + shift)
            tile_of = jnp.floor(source * (1.0 / LANES))
            inside = (source - LANES * tile_of).astype(jnp.int32)
            index = jnp.broadcast_to(inside, (count, LANES))
            for pair_block, tile in tile_pairs(outer):
                if pair_block != block:
                    continue
                term = jnp.where(tile_of == float(tile), coef, 0.0) * lane_take(tiles[tile], index)
                result[block] = term if result[block] is None else result[block] + term
    return result


def band_backward(blocks, step):
    outer, count = len(blocks), blocks[0].shape[0]
    lane = lax.broadcasted_iota(jnp.int32, (1, LANES), 1).astype(jnp.float32)
    center = float(outer // 2 * LANES)
    result = [None] * outer
    for tile in range(outer):
        target = (lane + (LANES * tile - center)) * 4096.0
        first = jnp.floor(target / step)
        for shift in (-1.0, 0.0, 1.0, 2.0):
            source = first + shift
            coef = jnp.maximum(4096.0 - jnp.abs(step * source - target), 0.0) * (1.0 / 4096.0)
            place = source + center
            block_of = jnp.floor(place * (1.0 / LANES))
            inside = (place - LANES * block_of).astype(jnp.int32)
            index = jnp.broadcast_to(inside, (count, LANES))
            for block, pair_tile in tile_pairs(outer):
                if pair_tile != tile:
                    continue
                term = jnp.where(block_of == float(block), coef, 0.0) * lane_take(blocks[block], index)
                result[tile] = term if result[tile] is None else result[tile] + term
    return result


def image_step(ray_tiles, slopes, fresnels, measured, tables, angles_total):
    forward, inverse, small, left, right, row_freq2 = tables
    angles, outer = len(ray_tiles), len(ray_tiles[0])
    slices = ray_tiles[0][0].shape[0]
    rows = angles * slices
    width = outer * LANES
    mix_cos, mix_sin, col_freq2 = small
    scales, steps = [], []
    for slope in slopes:
        value = slope.astype(jnp.float32)
        steps.append(value + 3072.0)
        tangent = jnp.full((1, LANES), value) * (1.0 / 512.0)
        scales.append(jnp.sqrt(1.0 + tangent * tangent))
    images = [band_forward(ray_tiles[a], steps[a]) for a in range(angles)]
    waves = []
    for q in range(outer):
        image = jnp.concatenate([images[a][q] * scales[a] for a in range(angles)], axis=0)
        fade = jnp.exp(-ABSORB * image)
        waves.append((fade * jnp.cos(image), fade * jnp.sin(image)))
    spectrum = columns_forward(waves, forward, mix_cos, mix_sin)
    spec_re = [spectrum[k * rows : (k + 1) * rows, :LANES] for k in range(outer)]
    spec_im = [spectrum[k * rows : (k + 1) * rows, LANES:] for k in range(outer)]
    total = [None] * outer
    for d in range(len(fresnels)):
        phase = (math.pi * fresnels[d]) * col_freq2
        col_cos, col_sin = jnp.cos(phase), jnp.sin(phase)
        row_phase = (math.pi * fresnels[d]) * row_freq2
        left_cos, left_sin = left[0] * jnp.cos(row_phase), left[1] * jnp.sin(row_phase)
        mix = dot(left_cos - left_sin, right)
        mix_back = dot(left_cos + left_sin, right)
        scaled = []
        for k in range(outer):
            c, s = col_cos[k : k + 1], col_sin[k : k + 1]
            re, im = spec_re[k], spec_im[k]
            scaled.append(jnp.concatenate([re * c + im * s, im * c - re * s], axis=1))
        parts = columns_inverse(jnp.concatenate(scaled, axis=0), inverse, mix_cos, mix_sin)
        stacked = jnp.concatenate([jnp.concatenate(part, axis=0) for part in parts], axis=1)
        field = dot(mix, stacked * (1.0 / width))
        re, im = field[:rows], field[rows:]
        slope_of = (re * re + im * im - measured[d]) * (4.0 / angles_total)
        back = dot(mix_back, jnp.concatenate([slope_of * re, slope_of * im], axis=0))
        pieces = [
            (back[:rows, q * LANES : (q + 1) * LANES], back[rows:, q * LANES : (q + 1) * LANES])
            for q in range(outer)
        ]
        adjoint = columns_forward(pieces, forward, mix_cos, mix_sin)
        for k in range(outer):
            c, s = col_cos[k : k + 1], col_sin[k : k + 1]
            re = adjoint[k * rows : (k + 1) * rows, :LANES]
            im = adjoint[k * rows : (k + 1) * rows, LANES:]
            term = jnp.concatenate([re * c - im * s, im * c + re * s], axis=1)
            total[k] = term if total[k] is None else total[k] + term
    parts = columns_inverse(jnp.concatenate(total, axis=0), inverse, mix_cos, mix_sin)
    grads = []
    for q in range(outer):
        (re, im), (wave_re, wave_im) = parts[q], waves[q]
        re, im = re * (1.0 / width), im * (1.0 / width)
        grads.append(re * (-ABSORB * wave_re - wave_im) + im * (wave_re - ABSORB * wave_im))
    result = []
    for a in range(angles):
        own = [g[a * slices : (a + 1) * slices] * scales[a] for g in grads]
        result.append(band_backward(own, steps[a]))
    return result


def fused_kernel(
    sizes, slope_ref, fresnel_ref, volume_hbm, weight_ref, measured_hbm,
    forward_ref, inverse_ref, small_ref, left_ref, right_ref, freq_ref, out_ref,
    volume_ref, own_ref, other_ref, fresnel_out, fresnel_in, send_ref, recv_ref, back_ref,
    local_sem, swap_send, swap_recv, send_sem, recv_sem, back_send, back_recv,
):
    angles, slices, outer, angles_total, rows_own, devices = sizes
    ang, dist = lax.axis_index("ang"), lax.axis_index("dist")
    me = ang * 2 + dist
    piece = angles * outer
    rows = angles * slices
    barrier = pltpu.get_barrier_semaphore()

    def place_of(step):
        there = lax.rem(me + step, devices)
        return there, (there // 2, lax.rem(there, 2))

    volume_copy = pltpu.make_async_copy(volume_hbm, volume_ref, local_sem.at[0])
    volume_copy.start()
    own_copy = pltpu.make_async_copy(
        measured_hbm.at[pl.ds(dist * angles, angles)], own_ref, local_sem.at[1]
    )
    own_copy.start()

    def greet(step, carry):
        pl.semaphore_signal(
            barrier, inc=1, device_id=place_of(step)[1], device_id_type=pl.DeviceIdType.MESH
        )
        return carry

    lax.fori_loop(1, devices, greet, 0)
    fresnel_out[...] = jnp.full(fresnel_out.shape, fresnel_ref[0])
    weights = weight_ref[:, pl.ds(pl.multiple_of(dist * rows_own, LANES), rows_own)]
    volume_copy.wait()
    for q in range(outer):
        send_ref[pl.ds(q, angles_total, outer), :] = dot(
            weights, volume_ref[:, q * LANES : (q + 1) * LANES]
        )
    pl.semaphore_wait(barrier, devices - 1)

    def send(step, carry):
        there, target = place_of(step)
        pltpu.make_async_remote_copy(
            src_ref=send_ref.at[pl.ds(there * piece, piece)],
            dst_ref=recv_ref.at[pl.ds(me * piece, piece)],
            send_sem=send_sem, recv_sem=recv_sem,
            device_id=target, device_id_type=pl.DeviceIdType.MESH,
        ).start()
        return carry

    lax.fori_loop(1, devices, send, 0)
    pltpu.make_async_copy(
        send_ref.at[pl.ds(me * piece, piece)], recv_ref.at[pl.ds(me * piece, piece)], recv_sem
    ).start()
    swaps = []
    for n, (source, target) in enumerate((
        (fresnel_out, fresnel_in),
        (measured_hbm.at[pl.ds((1 - dist) * angles, angles)], other_ref),
    )):
        swaps.append(pltpu.make_async_remote_copy(
            src_ref=source, dst_ref=target, send_sem=swap_send.at[n], recv_sem=swap_recv.at[n],
            device_id=(ang, 1 - dist), device_id_type=pl.DeviceIdType.MESH,
        ))
        swaps[n].start()
    own_copy.wait()
    for swap in swaps:
        swap.wait()
    fresnels = [fresnel_out[0:1, 0:1], fresnel_in[0:1, 0:1]]
    shift = devices - 1
    pltpu.make_async_copy(recv_ref, recv_ref, recv_sem).wait()
    part = send_ref.at[pl.ds(0, shift * piece)]
    pltpu.make_async_copy(part, part, send_sem).wait()
    stride = 2 * piece
    rays = []
    for a in range(angles):
        rays.append([
            recv_ref[pl.ds(a * outer + q, slices, stride), :]
            + recv_ref[pl.ds((angles + a) * outer + q, slices, stride), :]
            for q in range(outer)
        ])
    tables = (
        forward_ref[...], inverse_ref[...], (small_ref[0], small_ref[1], small_ref[2]),
        (left_ref[0], left_ref[1]), right_ref[...], freq_ref[...],
    )
    result = image_step(
        rays, [slope_ref[me * angles + a] for a in range(angles)], fresnels,
        [own_ref[...].reshape(rows, outer * LANES), other_ref[...].reshape(rows, outer * LANES)],
        tables, angles_total,
    )
    for a in range(angles):
        for q in range(outer):
            back_ref[pl.ds(a * outer + q, slices, piece), :] = result[a][q]

    def send_back(step, carry):
        there, target = place_of(step)
        pltpu.make_async_remote_copy(
            src_ref=back_ref.at[pl.ds((there // 2) * piece, piece)],
            dst_ref=out_ref.at[pl.ds(me * piece, piece)],
            send_sem=back_send, recv_sem=back_recv,
            device_id=target, device_id_type=pl.DeviceIdType.MESH,
        ).start()
        return carry

    lax.fori_loop(1, devices, send_back, 0)
    pltpu.make_async_copy(
        back_ref.at[pl.ds(ang * piece, piece)], out_ref.at[pl.ds(me * piece, piece)], back_recv
    ).start()
    pltpu.make_async_copy(out_ref, out_ref, back_recv).wait()
    sent = out_ref.at[pl.ds(0, shift * piece)]
    pltpu.make_async_copy(sent, sent, back_send).wait()


def fused_call(slopes, fresnel, volume, weights, measured):
    group, slices, width = measured.shape
    angles, outer = group // 2, width // LANES
    angles_total, rows_own = weights.shape[0], volume.shape[0]
    devices = angles_total // angles
    piece = angles * outer
    tables = column_tables(width) + row_tables(slices, angles)
    smem = pl.BlockSpec(memory_space=pltpu.SMEM)
    vmem = pl.BlockSpec(memory_space=pltpu.VMEM)
    hbm = pl.BlockSpec(memory_space=pl.ANY)
    f32 = jnp.float32
    dma = pltpu.SemaphoreType.DMA
    return pl.pallas_call(
        partial(fused_kernel, (angles, slices, outer, angles_total, rows_own, devices)),
        out_shape=jax.ShapeDtypeStruct((devices * piece, LANES), f32),
        in_specs=[smem, smem, hbm, vmem, hbm] + [vmem] * 6,
        out_specs=vmem,
        scratch_shapes=[
            pltpu.VMEM((rows_own, width), f32),
            pltpu.VMEM((angles, slices, width), f32),
            pltpu.VMEM((angles, slices, width), f32),
            pltpu.VMEM((8, LANES), f32),
            pltpu.VMEM((8, LANES), f32),
            pltpu.VMEM((devices * piece, LANES), f32),
            pltpu.VMEM((devices * piece, LANES), f32),
            pltpu.VMEM((slices * piece, LANES), f32),
            dma((2,)), dma((2,)), dma((2,)), dma, dma, dma, dma,
        ],
        compiler_params=pltpu.CompilerParams(
            vmem_limit_bytes=40 * 2**20, collective_id=0, has_side_effects=True
        ),
    )(slopes, fresnel, volume, weights, measured, *[jnp.asarray(t) for t in tables])


def shards(volume, row_weights, angle_slope, shear_index, shear_weight, fresnel, measured):
    row_count, width = volume.shape[1], volume.shape[2]
    own_weights = lax.dynamic_slice_in_dim(
        row_weights, lax.axis_index("dist") * row_count, row_count, 1
    )
    spread = fused_call(angle_slope, fresnel, volume[0], row_weights, measured[0])
    spread = spread.reshape(row_weights.shape[0], width)
    return jnp.einsum("ay,ax->yx", own_weights, spread, precision=HIGHEST)[None]


def solution(mesh):
    placed = (P("ang", "dist", None), P(), P(), P(), P(), P("dist"), P("dist", "ang", None, None))
    return jax.shard_map(
        shards, mesh=mesh, in_specs=placed, out_specs=P("ang", "dist", None), check_vma=False
    )
```

```python
from functools import partial
import math

import numpy as np
import jax
import jax.numpy as jnp
from jax import lax
from jax.experimental import pallas as pl
from jax.experimental.pallas import tpu as pltpu
from jax.sharding import PartitionSpec as P

ABSORB = 0.1
HIGHEST = lax.Precision.HIGHEST
LANES = 128


def dot(a, b):
    return lax.dot_general(
        a, b, (((1,), (0,)), ((), ())), precision=HIGHEST, preferred_element_type=jnp.float32
    )


def dot_narrow(a, b):
    return lax.dot_general(a, b, (((1,), (0,)), ((), ())), preferred_element_type=jnp.float32)


def halves(a):
    high = a.astype(jnp.bfloat16)
    return high, (a - high.astype(jnp.float32)).astype(jnp.bfloat16)


def dot_left(a, high, low):
    rows = a.shape[0]
    a_high, a_low = halves(a)
    both = dot_narrow(jnp.concatenate([a_high, a_low], axis=0), high)
    return both[:rows] + both[rows:] + dot_narrow(a_high, low)


def dot_right(table, table_high, b):
    rows = table_high.shape[0]
    b_high, b_low = halves(b)
    both = dot_narrow(table, b_high)
    return both[:rows] + both[rows:] + dot_narrow(table_high, b_low)


def signed_freq(counter, length):
    return np.where(counter <= (length - 1) // 2, counter, counter - length) / length


def column_tables(width):
    outer = width // LANES
    p = np.arange(LANES)
    k = np.arange(outer)
    ang = 2 * np.pi * (p[:, None] * p[None, :] % LANES) / LANES
    c, s = np.cos(ang), np.sin(ang)
    forward = np.block([[c, -s], [s, c]])
    high = forward.astype(jnp.bfloat16)
    low = (forward - high.astype(np.float64)).astype(jnp.bfloat16)
    mixed = 2 * np.pi * (k[:, None] * p[None, :] % width) / width
    freq2 = signed_freq(k[:, None] + outer * p[None, :], width) ** 2
    small = np.stack([np.cos(mixed), np.sin(mixed), freq2])
    return np.stack([high, low]), small.astype(np.float32)


def row_tables(slices, angles):
    z = np.arange(slices)
    ang = 2 * np.pi * (z[:, None] * z[None, :] % slices) / slices
    trig = np.stack([np.cos(ang), np.sin(ang)])
    rows = 2 * angles * slices
    left_r = np.zeros((2, angles, slices, 2, angles, 2, slices))
    left_i = np.zeros_like(left_r)
    right = np.zeros((2, angles, 2, slices, 2, angles, slices))
    for c in range(2):
        for a in range(angles):
            for t in range(2):
                left_r[c, a, :, c, a, t, :] = trig[t]
                left_i[c, a, :, 1 - c, a, t, :] = trig[t] * (-1.0 if c == 0 else 1.0)
                right[c, a, t, :, c, a, :] = trig[t] / slices
    freq2 = np.broadcast_to(signed_freq(z, slices) ** 2, (2, angles, 2, slices)).reshape(1, -1)
    left = np.stack([left_r.reshape(rows, -1), left_i.reshape(rows, -1)])
    return left.astype(np.float32), right.reshape(-1, rows).astype(np.float32), freq2.astype(np.float32)


def fft_list(parts, sign):
    n = len(parts)
    if n == 1:
        return parts
    even = fft_list(parts[0::2], sign)
    odd = fft_list(parts[1::2], sign)
    low, high = [], []
    for k in range(n // 2):
        (er, ei), (br, bi) = even[k], odd[k]
        if k == 0:
            tr, ti = br, bi
        elif 4 * k == n:
            tr, ti = (-bi, br) if sign > 0 else (bi, -br)
        else:
            wr = math.cos(2 * math.pi * k / n)
            wi = sign * math.sin(2 * math.pi * k / n)
            tr, ti = br * wr - bi * wi, br * wi + bi * wr
        low.append((er + tr, ei + ti))
        high.append((er - tr, ei - ti))
    return low + high


def columns_forward(parts, table, mix_cos, mix_sin):
    parts = fft_list(parts, -1)
    rows = []
    for k, (re, im) in enumerate(parts):
        c, s = mix_cos[k : k + 1], mix_sin[k : k + 1]
        rows.append(jnp.concatenate([re * c + im * s, im * c - re * s], axis=1))
    return dot_left(jnp.concatenate(rows, axis=0), *table)


def columns_inverse(spectrum, table, mix_cos, mix_sin):
    outer = mix_cos.shape[0]
    count = spectrum.shape[0] // outer
    result = dot_left(spectrum, *table)
    parts = []
    for k in range(outer):
        im = result[k * count : (k + 1) * count, :LANES]
        re = result[k * count : (k + 1) * count, LANES:]
        c, s = mix_cos[k : k + 1], mix_sin[k : k + 1]
        parts.append((re * c - im * s, im * c + re * s))
    return fft_list(parts, 1)


def tile_pairs(outer):
    pairs = []
    half = outer // 2
    for block in range(outer):
        first = LANES * (block - half)
        ends = [first, first + LANES - 1]
        low = min(min(math.floor(u * 0.5), math.floor(u * 4095 / 4096)) for u in ends)
        high = max(max(math.floor(u * 0.5), math.floor(u * 4095 / 4096)) for u in ends) + 1
        for tile in range(low // LANES + half, high // LANES + half + 1):
            if 0 <= tile < outer:
                pairs.append((block, tile))
    return pairs


def lane_take(values, index):
    return jnp.take_along_axis(values, index, axis=1, mode="promise_in_bounds")


def band_forward(tiles, step):
    outer, count = len(tiles), tiles[0].shape[0]
    lane = lax.broadcasted_iota(jnp.int32, (1, LANES), 1).astype(jnp.float32)
    center = float(outer // 2 * LANES)
    result = [None] * outer
    for block in range(outer):
        place = step * (lane + (LANES * block - center)) * (1.0 / 4096.0)
        lower = jnp.floor(place)
        weight = place - lower
        for shift, coef in ((0.0, 1.0 - weight), (1.0, weight)):
            source = lower + (center + shift)
            tile_of = jnp.floor(source * (1.0 / LANES))
            inside = (source - LANES * tile_of).astype(jnp.int32)
            index = jnp.broadcast_to(inside, (count, LANES))
            for pair_block, tile in tile_pairs(outer):
                if pair_block != block:
                    continue
                term = jnp.where(tile_of == float(tile), coef, 0.0) * lane_take(tiles[tile], index)
                result[block] = term if result[block] is None else result[block] + term
    return result


def band_backward(blocks, step):
    outer, count = len(blocks), blocks[0].shape[0]
    lane = lax.broadcasted_iota(jnp.int32, (1, LANES), 1).astype(jnp.float32)
    center = float(outer // 2 * LANES)
    result = [None] * outer
    for tile in range(outer):
        target = (lane + (LANES * tile - center)) * 4096.0
        first = jnp.floor(target / step)
        for shift in (-1.0, 0.0, 1.0, 2.0):
            source = first + shift
            coef = jnp.maximum(4096.0 - jnp.abs(step * source - target), 0.0) * (1.0 / 4096.0)
            place = source + center
            block_of = jnp.floor(place * (1.0 / LANES))
            inside = (place - LANES * block_of).astype(jnp.int32)
            index = jnp.broadcast_to(inside, (count, LANES))
            for block, pair_tile in tile_pairs(outer):
                if pair_tile != tile:
                    continue
                term = jnp.where(block_of == float(block), coef, 0.0) * lane_take(blocks[block], index)
                result[tile] = term if result[tile] is None else result[tile] + term
    return result


def image_step(ray_tiles, slopes, fresnels, measured, tables, angles_total):
    forward, small, left, right, row_freq2 = tables
    angles, outer = len(ray_tiles), len(ray_tiles[0])
    slices = ray_tiles[0][0].shape[0]
    rows = angles * slices
    width = outer * LANES
    mix_cos, mix_sin, col_freq2 = small
    scales, steps = [], []
    for slope in slopes:
        value = slope.astype(jnp.float32)
        steps.append(value + 3072.0)
        tangent = jnp.full((1, LANES), value) * (1.0 / 512.0)
        scales.append(jnp.sqrt(1.0 + tangent * tangent))
    images = [band_forward(ray_tiles[a], steps[a]) for a in range(angles)]
    waves = []
    for q in range(outer):
        image = jnp.concatenate([images[a][q] * scales[a] for a in range(angles)], axis=0)
        fade = jnp.exp(-ABSORB * image)
        waves.append((fade * jnp.cos(image), fade * jnp.sin(image)))
    spectrum = columns_forward(waves, forward, mix_cos, mix_sin)
    spec_re = [spectrum[k * rows : (k + 1) * rows, :LANES] for k in range(outer)]
    spec_im = [spectrum[k * rows : (k + 1) * rows, LANES:] for k in range(outer)]
    total = [None] * outer
    for d in range(len(fresnels)):
        phase = (math.pi * fresnels[d]) * col_freq2
        col_cos, col_sin = jnp.cos(phase), jnp.sin(phase)
        row_phase = (math.pi * fresnels[d]) * row_freq2
        left_cos, left_sin = left[0] * jnp.cos(row_phase), left[1] * jnp.sin(row_phase)
        mix = jnp.concatenate(halves(dot(left_cos - left_sin, right)), axis=0)
        mix_back = jnp.concatenate(halves(dot(left_cos + left_sin, right)), axis=0)
        scaled = []
        for k in range(outer):
            c, s = col_cos[k : k + 1], col_sin[k : k + 1]
            re, im = spec_re[k], spec_im[k]
            scaled.append(jnp.concatenate([im * c - re * s, re * c + im * s], axis=1))
        parts = columns_inverse(jnp.concatenate(scaled, axis=0), forward, mix_cos, mix_sin)
        stacked = jnp.concatenate([jnp.concatenate(part, axis=0) for part in parts], axis=1)
        field = dot_right(mix, mix[: 2 * rows], stacked * (1.0 / width))
        re, im = field[:rows], field[rows:]
        slope_of = (re * re + im * im - measured[d]) * (4.0 / angles_total)
        back = dot_right(mix_back, mix_back[: 2 * rows], jnp.concatenate([slope_of * re, slope_of * im], axis=0))
        pieces = [
            (back[:rows, q * LANES : (q + 1) * LANES], back[rows:, q * LANES : (q + 1) * LANES])
            for q in range(outer)
        ]
        adjoint = columns_forward(pieces, forward, mix_cos, mix_sin)
        for k in range(outer):
            c, s = col_cos[k : k + 1], col_sin[k : k + 1]
            re = adjoint[k * rows : (k + 1) * rows, :LANES]
            im = adjoint[k * rows : (k + 1) * rows, LANES:]
            term = jnp.concatenate([im * c + re * s, re * c - im * s], axis=1)
            total[k] = term if total[k] is None else total[k] + term
    parts = columns_inverse(jnp.concatenate(total, axis=0), forward, mix_cos, mix_sin)
    grads = []
    for q in range(outer):
        (re, im), (wave_re, wave_im) = parts[q], waves[q]
        re, im = re * (1.0 / width), im * (1.0 / width)
        grads.append(re * (-ABSORB * wave_re - wave_im) + im * (wave_re - ABSORB * wave_im))
    result = []
    for a in range(angles):
        own = [g[a * slices : (a + 1) * slices] * scales[a] for g in grads]
        result.append(band_backward(own, steps[a]))
    return result


def fused_kernel(
    sizes, slope_ref, fresnel_ref, volume_hbm, weight_hbm, measured_hbm,
    forward_hbm, small_hbm, left_hbm, right_hbm, freq_hbm, spread_ref, stack_ref,
    weight_ref, forward_ref, small_ref, left_ref, right_ref, freq_ref, out_ref,
    volume_ref, own_ref, other_ref, fresnel_out, fresnel_in, send_ref, recv_ref, back_ref,
    local_sem, swap_send, swap_recv, send_sem, recv_sem, back_send, back_recv,
):
    angles, slices, outer, angles_total, rows_own, devices = sizes
    ang, dist = lax.axis_index("ang"), lax.axis_index("dist")
    me = ang * 2 + dist
    piece = angles * outer
    rows = angles * slices
    barrier = pltpu.get_barrier_semaphore()

    def place_of(step):
        there = lax.rem(me + step, devices)
        return there, (there // 2, lax.rem(there, 2))

    weight_copy = pltpu.make_async_copy(
        weight_hbm.at[:, pl.ds(pl.multiple_of(dist * rows_own, LANES), rows_own)],
        weight_ref, local_sem.at[2],
    )
    weight_copy.start()
    volume_copy = pltpu.make_async_copy(volume_hbm, volume_ref, local_sem.at[0])
    volume_copy.start()
    own_copy = pltpu.make_async_copy(
        measured_hbm.at[pl.ds(dist * angles, angles)], own_ref, local_sem.at[1]
    )
    own_copy.start()
    table_copies = []
    for n, (source, target) in enumerate((
        (forward_hbm, forward_ref), (small_hbm, small_ref), (left_hbm, left_ref),
        (right_hbm, right_ref), (freq_hbm, freq_ref),
    )):
        table_copies.append(pltpu.make_async_copy(source, target, local_sem.at[3 + n]))
        table_copies[n].start()

    def greet(step, carry):
        pl.semaphore_signal(
            barrier, inc=1, device_id=place_of(step)[1], device_id_type=pl.DeviceIdType.MESH
        )
        return carry

    lax.fori_loop(1, devices, greet, 0)
    fresnel_out[...] = jnp.full(fresnel_out.shape, fresnel_ref[0])
    weight_copy.wait()
    weight_high, weight_low = halves(weight_ref[...])
    weights = jnp.concatenate([weight_high, weight_low], axis=0)
    stack_ref[...] = jnp.concatenate([weight_high, weight_low, weight_high], axis=0)
    volume_copy.wait()
    for q in range(0, outer, 2):
        high, low = halves(volume_ref[:, q * LANES : (q + 2) * LANES])
        both = dot_narrow(weights, high) + dot_narrow(weights, low)
        total = both[:angles_total] + both[angles_total:]
        send_ref[pl.ds(q, angles_total, outer), :] = total[:, :LANES]
        send_ref[pl.ds(q + 1, angles_total, outer), :] = total[:, LANES:]
    pl.semaphore_wait(barrier, devices - 1)

    def send(step, carry):
        there, target = place_of(step)
        pltpu.make_async_remote_copy(
            src_ref=send_ref.at[pl.ds(there * piece, piece)],
            dst_ref=recv_ref.at[pl.ds(me * piece, piece)],
            send_sem=send_sem, recv_sem=recv_sem,
            device_id=target, device_id_type=pl.DeviceIdType.MESH,
        ).start()
        return carry

    lax.fori_loop(1, devices, send, 0)
    pltpu.make_async_copy(
        send_ref.at[pl.ds(me * piece, piece)], recv_ref.at[pl.ds(me * piece, piece)], recv_sem
    ).start()
    swaps = []
    for n, (source, target) in enumerate((
        (fresnel_out, fresnel_in),
        (measured_hbm.at[pl.ds((1 - dist) * angles, angles)], other_ref),
    )):
        swaps.append(pltpu.make_async_remote_copy(
            src_ref=source, dst_ref=target, send_sem=swap_send.at[n], recv_sem=swap_recv.at[n],
            device_id=(ang, 1 - dist), device_id_type=pl.DeviceIdType.MESH,
        ))
        swaps[n].start()
    own_copy.wait()
    for copy in table_copies:
        copy.wait()
    for swap in swaps:
        swap.wait()
    fresnels = [fresnel_out[0:1, 0:1], fresnel_in[0:1, 0:1]]
    shift = devices - 1
    pltpu.make_async_copy(recv_ref, recv_ref, recv_sem).wait()
    part = send_ref.at[pl.ds(0, shift * piece)]
    pltpu.make_async_copy(part, part, send_sem).wait()
    stride = 2 * piece
    rays = []
    for a in range(angles):
        rays.append([
            recv_ref[pl.ds(a * outer + q, slices, stride), :]
            + recv_ref[pl.ds((angles + a) * outer + q, slices, stride), :]
            for q in range(outer)
        ])
    tables = (
        (forward_ref[0], forward_ref[1]), (small_ref[0], small_ref[1], small_ref[2]),
        (left_ref[0], left_ref[1]), right_ref[...], freq_ref[...],
    )
    result = image_step(
        rays, [slope_ref[me * angles + a] for a in range(angles)], fresnels,
        [own_ref[...].reshape(rows, outer * LANES), other_ref[...].reshape(rows, outer * LANES)],
        tables, angles_total,
    )
    for a in range(angles):
        for q in range(outer):
            back_ref[pl.ds(a * outer + q, slices, piece), :] = result[a][q]

    def send_back(step, carry):
        there, target = place_of(step)
        pltpu.make_async_remote_copy(
            src_ref=back_ref.at[pl.ds((there // 2) * piece, piece)],
            dst_ref=out_ref.at[pl.ds(me * piece, piece)],
            send_sem=back_send, recv_sem=back_recv,
            device_id=target, device_id_type=pl.DeviceIdType.MESH,
        ).start()
        return carry

    lax.fori_loop(1, devices, send_back, 0)
    pltpu.make_async_copy(
        back_ref.at[pl.ds(ang * piece, piece)], out_ref.at[pl.ds(me * piece, piece)], back_recv
    ).start()
    pltpu.make_async_copy(out_ref, out_ref, back_recv).wait()
    sent = out_ref.at[pl.ds(0, shift * piece)]
    pltpu.make_async_copy(sent, sent, back_send).wait()
    for q in range(outer):
        high, low = halves(out_ref[pl.ds(q, angles_total, outer), :])
        spread_ref[:, q * LANES : (q + 1) * LANES] = jnp.concatenate([high, high, low], axis=0)


def fused_call(slopes, fresnel, volume, weights, measured):
    group, slices, width = measured.shape
    angles, outer = group // 2, width // LANES
    angles_total, rows_own = weights.shape[0], volume.shape[0]
    devices = angles_total // angles
    piece = angles * outer
    tables = column_tables(width) + row_tables(slices, angles)
    smem = pl.BlockSpec(memory_space=pltpu.SMEM)
    vmem = pl.BlockSpec(memory_space=pltpu.VMEM)
    hbm = pl.BlockSpec(memory_space=pl.ANY)
    f32 = jnp.float32
    dma = pltpu.SemaphoreType.DMA
    return pl.pallas_call(
        partial(fused_kernel, (angles, slices, outer, angles_total, rows_own, devices)),
        out_shape=(
            jax.ShapeDtypeStruct((3 * angles_total, width), jnp.bfloat16),
            jax.ShapeDtypeStruct((3 * angles_total, rows_own), jnp.bfloat16),
        ),
        in_specs=[smem, smem] + [hbm] * 8,
        out_specs=(vmem, vmem),
        scratch_shapes=[
            pltpu.VMEM((angles_total, rows_own), f32),
            *[pltpu.VMEM(t.shape, t.dtype) for t in tables],
            pltpu.VMEM((devices * piece, LANES), f32),
            pltpu.VMEM((rows_own, width), f32),
            pltpu.VMEM((angles, slices, width), f32),
            pltpu.VMEM((angles, slices, width), f32),
            pltpu.VMEM((8, LANES), f32),
            pltpu.VMEM((8, LANES), f32),
            pltpu.VMEM((devices * piece, LANES), f32),
            pltpu.VMEM((devices * piece, LANES), f32),
            pltpu.VMEM((slices * piece, LANES), f32),
            dma((8,)), dma((2,)), dma((2,)), dma, dma, dma, dma,
        ],
        compiler_params=pltpu.CompilerParams(
            vmem_limit_bytes=58 * 2**20, collective_id=0, has_side_effects=True
        ),
    )(slopes, fresnel, volume, weights, measured, *[jnp.asarray(t) for t in tables])


def shards(volume, row_weights, angle_slope, shear_index, shear_weight, fresnel, measured):
    spread, weights = fused_call(angle_slope, fresnel, volume[0], row_weights, measured[0])
    return jnp.einsum("ky,kx->yx", weights, spread, preferred_element_type=jnp.float32)[None]


def solution(mesh):
    placed = (P("ang", "dist", None), P(), P(), P(), P(), P("dist"), P("dist", "ang", None, None))
    return jax.shard_map(
        shards, mesh=mesh, in_specs=placed, out_specs=P("ang", "dist", None), check_vma=False
    )
```

```python
from functools import partial
import math

import numpy as np
import jax
import jax.numpy as jnp
from jax import lax
from jax.experimental import pallas as pl
from jax.experimental.pallas import tpu as pltpu
from jax.sharding import PartitionSpec as P

ABSORB = 0.1
HIGHEST = lax.Precision.HIGHEST
LANES = 128


def dot(a, b):
    return lax.dot_general(
        a, b, (((1,), (0,)), ((), ())), precision=HIGHEST, preferred_element_type=jnp.float32
    )


def dot_narrow(a, b):
    return lax.dot_general(a, b, (((1,), (0,)), ((), ())), preferred_element_type=jnp.float32)


def halves(a):
    high = a.astype(jnp.bfloat16)
    return high, (a - high.astype(jnp.float32)).astype(jnp.bfloat16)


def dot_left(a, high, low):
    rows = a.shape[0]
    a_high, a_low = halves(a)
    both = dot_narrow(jnp.concatenate([a_high, a_low], axis=0), high)
    return both[:rows] + both[rows:] + dot_narrow(a_high, low)


def dot_right(table, table_high, b):
    rows = table_high.shape[0]
    b_high, b_low = halves(b)
    both = dot_narrow(table, b_high)
    return both[:rows] + both[rows:] + dot_narrow(table_high, b_low)


def signed_freq(counter, length):
    return np.where(counter <= (length - 1) // 2, counter, counter - length) / length


def column_tables(width):
    outer = width // LANES
    p = np.arange(LANES)
    k = np.arange(outer)
    ang = 2 * np.pi * (p[:, None] * p[None, :] % LANES) / LANES
    c, s = np.cos(ang), np.sin(ang)
    forward = np.block([[c, -s], [s, c]])
    high = forward.astype(jnp.bfloat16)
    low = (forward - high.astype(np.float64)).astype(jnp.bfloat16)
    mixed = 2 * np.pi * (k[:, None] * p[None, :] % width) / width
    freq2 = signed_freq(k[:, None] + outer * p[None, :], width) ** 2
    small = np.stack([np.cos(mixed), np.sin(mixed), freq2])
    return np.stack([high, low]), small.astype(np.float32)


def row_tables(slices, angles):
    z = np.arange(slices)
    ang = 2 * np.pi * (z[:, None] * z[None, :] % slices) / slices
    trig = np.stack([np.cos(ang), np.sin(ang)])
    rows = 2 * angles * slices
    left_r = np.zeros((2, angles, slices, 2, angles, 2, slices))
    left_i = np.zeros_like(left_r)
    right = np.zeros((2, angles, 2, slices, 2, angles, slices))
    for c in range(2):
        for a in range(angles):
            for t in range(2):
                left_r[c, a, :, c, a, t, :] = trig[t]
                left_i[c, a, :, 1 - c, a, t, :] = trig[t] * (-1.0 if c == 0 else 1.0)
                right[c, a, t, :, c, a, :] = trig[t] / slices
    freq2 = np.broadcast_to(signed_freq(z, slices) ** 2, (2, angles, 2, slices)).reshape(1, -1)
    left = np.stack([left_r.reshape(rows, -1), left_i.reshape(rows, -1)])
    return left.astype(np.float32), right.reshape(-1, rows).astype(np.float32), freq2.astype(np.float32)


def fft_list(parts, sign):
    n = len(parts)
    if n == 1:
        return parts
    even = fft_list(parts[0::2], sign)
    odd = fft_list(parts[1::2], sign)
    low, high = [], []
    for k in range(n // 2):
        (er, ei), (br, bi) = even[k], odd[k]
        if k == 0:
            tr, ti = br, bi
        elif 4 * k == n:
            tr, ti = (-bi, br) if sign > 0 else (bi, -br)
        else:
            wr = math.cos(2 * math.pi * k / n)
            wi = sign * math.sin(2 * math.pi * k / n)
            tr, ti = br * wr - bi * wi, br * wi + bi * wr
        low.append((er + tr, ei + ti))
        high.append((er - tr, ei - ti))
    return low + high


def columns_forward(parts, table, mix_cos, mix_sin):
    parts = fft_list(parts, -1)
    rows = []
    for k, (re, im) in enumerate(parts):
        c, s = mix_cos[k : k + 1], mix_sin[k : k + 1]
        rows.append(jnp.concatenate([re * c + im * s, im * c - re * s], axis=1))
    return dot_left(jnp.concatenate(rows, axis=0), *table)


def columns_inverse(spectrum, table, mix_cos, mix_sin):
    outer = mix_cos.shape[0]
    count = spectrum.shape[0] // outer
    result = dot_left(spectrum, *table)
    parts = []
    for k in range(outer):
        im = result[k * count : (k + 1) * count, :LANES]
        re = result[k * count : (k + 1) * count, LANES:]
        c, s = mix_cos[k : k + 1], mix_sin[k : k + 1]
        parts.append((re * c - im * s, im * c + re * s))
    return fft_list(parts, 1)


def tile_pairs(outer):
    pairs = []
    half = outer // 2
    for block in range(outer):
        first = LANES * (block - half)
        ends = [first, first + LANES - 1]
        low = min(min(math.floor(u * 0.5), math.floor(u * 4095 / 4096)) for u in ends)
        high = max(max(math.floor(u * 0.5), math.floor(u * 4095 / 4096)) for u in ends) + 1
        for tile in range(low // LANES + half, high // LANES + half + 1):
            if 0 <= tile < outer:
                pairs.append((block, tile))
    return pairs


def lane_take(values, index):
    return jnp.take_along_axis(values, index, axis=1, mode="promise_in_bounds")


def band_forward(tiles, step):
    outer, count = len(tiles), tiles[0].shape[0]
    lane = lax.broadcasted_iota(jnp.int32, (1, LANES), 1).astype(jnp.float32)
    center = float(outer // 2 * LANES)
    result = [None] * outer
    for block in range(outer):
        place = step * (lane + (LANES * block - center)) * (1.0 / 4096.0)
        lower = jnp.floor(place)
        weight = place - lower
        for shift, coef in ((0.0, 1.0 - weight), (1.0, weight)):
            source = lower + (center + shift)
            tile_of = jnp.floor(source * (1.0 / LANES))
            inside = (source - LANES * tile_of).astype(jnp.int32)
            index = jnp.broadcast_to(inside, (count, LANES))
            for pair_block, tile in tile_pairs(outer):
                if pair_block != block:
                    continue
                term = jnp.where(tile_of == float(tile), coef, 0.0) * lane_take(tiles[tile], index)
                result[block] = term if result[block] is None else result[block] + term
    return result


def band_backward(blocks, step):
    outer, count = len(blocks), blocks[0].shape[0]
    lane = lax.broadcasted_iota(jnp.int32, (1, LANES), 1).astype(jnp.float32)
    center = float(outer // 2 * LANES)
    result = [None] * outer
    for tile in range(outer):
        target = (lane + (LANES * tile - center)) * 4096.0
        first = jnp.floor(target / step)
        for shift in (-1.0, 0.0, 1.0, 2.0):
            source = first + shift
            coef = jnp.maximum(4096.0 - jnp.abs(step * source - target), 0.0) * (1.0 / 4096.0)
            place = source + center
            block_of = jnp.floor(place * (1.0 / LANES))
            inside = (place - LANES * block_of).astype(jnp.int32)
            index = jnp.broadcast_to(inside, (count, LANES))
            for block, pair_tile in tile_pairs(outer):
                if pair_tile != tile:
                    continue
                term = jnp.where(block_of == float(block), coef, 0.0) * lane_take(blocks[block], index)
                result[tile] = term if result[tile] is None else result[tile] + term
    return result


def image_step(ray_tiles, slopes, fresnels, measured, tables, angles_total):
    forward, small, left, right, row_freq2 = tables
    angles, outer = len(ray_tiles), len(ray_tiles[0])
    slices = ray_tiles[0][0].shape[0]
    rows = angles * slices
    width = outer * LANES
    mix_cos, mix_sin, col_freq2 = small
    scales, steps = [], []
    for slope in slopes:
        value = slope.astype(jnp.float32)
        steps.append(value + 3072.0)
        tangent = jnp.full((1, LANES), value) * (1.0 / 512.0)
        scales.append(jnp.sqrt(1.0 + tangent * tangent))
    images = [band_forward(ray_tiles[a], steps[a]) for a in range(angles)]
    waves = []
    for q in range(outer):
        image = jnp.concatenate([images[a][q] * scales[a] for a in range(angles)], axis=0)
        fade = jnp.exp(-ABSORB * image)
        waves.append((fade * jnp.cos(image), fade * jnp.sin(image)))
    spectrum = columns_forward(waves, forward, mix_cos, mix_sin)
    spec_re = [spectrum[k * rows : (k + 1) * rows, :LANES] for k in range(outer)]
    spec_im = [spectrum[k * rows : (k + 1) * rows, LANES:] for k in range(outer)]
    total = [None] * outer
    for d in range(len(fresnels)):
        phase = (math.pi * fresnels[d]) * col_freq2
        col_cos, col_sin = jnp.cos(phase), jnp.sin(phase)
        row_phase = (math.pi * fresnels[d]) * row_freq2
        left_cos, left_sin = left[0] * jnp.cos(row_phase), left[1] * jnp.sin(row_phase)
        mix = jnp.concatenate(halves(dot(left_cos - left_sin, right)), axis=0)
        mix_back = jnp.concatenate(halves(dot(left_cos + left_sin, right)), axis=0)
        scaled = []
        for k in range(outer):
            c, s = col_cos[k : k + 1], col_sin[k : k + 1]
            re, im = spec_re[k], spec_im[k]
            scaled.append(jnp.concatenate([im * c - re * s, re * c + im * s], axis=1))
        parts = columns_inverse(jnp.concatenate(scaled, axis=0), forward, mix_cos, mix_sin)
        stacked = jnp.concatenate([jnp.concatenate(part, axis=0) for part in parts], axis=1)
        field = dot_right(mix, mix[: 2 * rows], stacked * (1.0 / width))
        re, im = field[:rows], field[rows:]
        slope_of = (re * re + im * im - measured[d]()) * (4.0 / angles_total)
        back = dot_right(mix_back, mix_back[: 2 * rows], jnp.concatenate([slope_of * re, slope_of * im], axis=0))
        pieces = [
            (back[:rows, q * LANES : (q + 1) * LANES], back[rows:, q * LANES : (q + 1) * LANES])
            for q in range(outer)
        ]
        adjoint = columns_forward(pieces, forward, mix_cos, mix_sin)
        for k in range(outer):
            c, s = col_cos[k : k + 1], col_sin[k : k + 1]
            re = adjoint[k * rows : (k + 1) * rows, :LANES]
            im = adjoint[k * rows : (k + 1) * rows, LANES:]
            term = jnp.concatenate([im * c + re * s, re * c - im * s], axis=1)
            total[k] = term if total[k] is None else total[k] + term
    parts = columns_inverse(jnp.concatenate(total, axis=0), forward, mix_cos, mix_sin)
    grads = []
    for q in range(outer):
        (re, im), (wave_re, wave_im) = parts[q], waves[q]
        re, im = re * (1.0 / width), im * (1.0 / width)
        grads.append(re * (-ABSORB * wave_re - wave_im) + im * (wave_re - ABSORB * wave_im))
    result = []
    for a in range(angles):
        own = [g[a * slices : (a + 1) * slices] * scales[a] for g in grads]
        result.append(band_backward(own, steps[a]))
    return result


def fused_kernel(
    sizes, slope_ref, fresnel_ref, volume_hbm, weight_hbm, measured_hbm,
    forward_hbm, small_hbm, left_hbm, right_hbm, freq_hbm, spread_ref, stack_hbm,
    weight_ref, forward_ref, small_ref, left_ref, right_ref, freq_ref, out_ref, stack_ref,
    volume_ref, own_ref, other_ref, fresnel_out, fresnel_in, keep_ref, give_ref, peer_ref,
    recv_ref, back_ref,
    local_sem, swap_send, swap_recv, peer_send, peer_recv, send_sem, recv_sem,
    back_send, back_recv, pass_send, pass_recv, weight_sem,
):
    angles, slices, outer, angles_total, rows_own, groups = sizes
    ang, dist = lax.axis_index("ang"), lax.axis_index("dist")
    me = ang * 2 + dist
    piece = angles * outer
    rows = angles * slices
    half = groups // 2
    chunk = half * piece
    partner = (ang, 1 - dist)
    mesh_ids = pl.DeviceIdType.MESH
    barrier = pltpu.get_barrier_semaphore()

    weight_copies = []
    for n in range(rows_own // LANES):
        first_row = pl.multiple_of(dist * rows_own + n * LANES, LANES)
        weight_copies.append(pltpu.make_async_copy(
            weight_hbm.at[:, pl.ds(first_row, LANES)],
            weight_ref.at[pl.ds(n * angles_total, angles_total)], weight_sem.at[n],
        ))
        weight_copies[n].start()
    volume_copy = pltpu.make_async_copy(volume_hbm, volume_ref, local_sem.at[0])
    volume_copy.start()
    own_copy = pltpu.make_async_copy(
        measured_hbm.at[pl.ds(dist * angles, angles)], own_ref, local_sem.at[1]
    )
    own_copy.start()
    table_copies = []
    for n, (source, target) in enumerate((
        (forward_hbm, forward_ref), (small_hbm, small_ref), (left_hbm, left_ref),
        (right_hbm, right_ref), (freq_hbm, freq_ref),
    )):
        table_copies.append(pltpu.make_async_copy(source, target, local_sem.at[3 + n]))
        table_copies[n].start()
    pl.semaphore_signal(barrier, inc=1, device_id=partner, device_id_type=mesh_ids)

    def greet(step, carry):
        there = lax.rem(ang + step, groups)
        pl.semaphore_signal(barrier, inc=1, device_id=(there, dist), device_id_type=mesh_ids)
        return carry

    lax.fori_loop(1, groups, greet, 0)
    fresnel_out[...] = jnp.full(fresnel_out.shape, fresnel_ref[0])
    for copy in weight_copies:
        copy.wait()
    columns = []
    for n in range(rows_own // LANES):
        blocks = []
        for which in (dist, 1 - dist):
            for a in range(angles):
                for c in range(2):
                    start = n * angles_total + c * 2 * angles + which * angles + a
                    blocks.append(weight_ref[pl.ds(start, half, 4 * angles), :])
        columns.append(jnp.concatenate(blocks, axis=0))
    ordered = jnp.concatenate(columns, axis=1)
    weight_high, weight_low = halves(ordered)
    weights = jnp.concatenate([weight_high, weight_low], axis=0)
    volume_copy.wait()
    for q in range(0, outer, 2):
        high, low = halves(volume_ref[:, q * LANES : (q + 2) * LANES])
        both = dot_narrow(weights, high) + dot_narrow(weights, low)
        total = both[:angles_total] + both[angles_total:]
        for rel, ref in enumerate((keep_ref, give_ref)):
            for a in range(angles):
                for c in range(2):
                    first = ((rel * angles + a) * 2 + c) * half
                    for p in range(2):
                        place = c * chunk + a * outer + q + p
                        ref[pl.ds(place, half, piece), :] = total[
                            first : first + half, p * LANES : (p + 1) * LANES
                        ]
    pl.semaphore_wait(barrier, groups)

    swaps = []
    for n, (source, target) in enumerate((
        (fresnel_out, fresnel_in),
        (measured_hbm.at[pl.ds((1 - dist) * angles, angles)], other_ref),
    )):
        swaps.append(pltpu.make_async_remote_copy(
            src_ref=source, dst_ref=target, send_sem=swap_send.at[n], recv_sem=swap_recv.at[n],
            device_id=partner, device_id_type=mesh_ids,
        ))
    peers = []
    for c in range(2):
        part = pl.ds(c * chunk, chunk)
        peers.append(pltpu.make_async_remote_copy(
            src_ref=give_ref.at[part], dst_ref=peer_ref.at[part],
            send_sem=peer_send.at[c], recv_sem=peer_recv.at[c],
            device_id=partner, device_id_type=mesh_ids,
        ))
        peers[c].start()
    swaps[0].start()
    swaps[1].start()

    pad = stack_ref.shape[1] - 3 * angles_total
    high_wide = weight_high.astype(jnp.float32)
    tall = [high_wide, weight_low.astype(jnp.float32), high_wide]
    if pad:
        tall.append(jnp.zeros((pad, rows_own), jnp.float32))
        spread_ref[3 * angles_total :, :] = jnp.zeros((pad, outer * LANES), jnp.bfloat16)
    stack_ref[...] = jnp.concatenate(tall, axis=0).T.astype(jnp.bfloat16)
    stack_copy = pltpu.make_async_copy(stack_ref, stack_hbm, local_sem.at[8])
    stack_copy.start()

    for c in range(2):
        peers[c].wait()
        part = pl.ds(c * chunk, chunk)
        keep_ref[part, :] = keep_ref[part, :] + peer_ref[part, :]

        def send(j):
            there = lax.rem(ang // 2 + j, half)
            return pltpu.make_async_remote_copy(
                src_ref=keep_ref.at[pl.ds(c * chunk + there * piece, piece)],
                dst_ref=recv_ref.at[pl.ds(ang * piece, piece)],
                send_sem=send_sem, recv_sem=recv_sem,
                device_id=(there * 2 + c, dist), device_id_type=mesh_ids,
            )

        def send_step(j, carry):
            send(j).start()
            return carry

        lax.fori_loop(1, half, send_step, 0)

        @pl.when(lax.rem(ang, 2) != c)
        def _():
            send(0).start()

        @pl.when(lax.rem(ang, 2) == c)
        def _():
            pltpu.make_async_copy(
                keep_ref.at[pl.ds(c * chunk + (ang // 2) * piece, piece)],
                recv_ref.at[pl.ds(ang * piece, piece)], recv_sem,
            ).start()

    own_copy.wait()
    for copy in table_copies:
        copy.wait()
    swaps[0].wait()
    fresnels = [fresnel_out[0:1, 0:1], fresnel_in[0:1, 0:1]]
    pltpu.make_async_copy(recv_ref, recv_ref, recv_sem).wait()
    rays = [
        [recv_ref[pl.ds(a * outer + q, slices, piece), :] for q in range(outer)]
        for a in range(angles)
    ]
    tables = (
        (forward_ref[0], forward_ref[1]), (small_ref[0], small_ref[1], small_ref[2]),
        (left_ref[0], left_ref[1]), right_ref[...], freq_ref[...],
    )

    def other_measured():
        swaps[1].wait()
        return other_ref[...].reshape(rows, outer * LANES)

    result = image_step(
        rays, [slope_ref[me * angles + a] for a in range(angles)], fresnels,
        [lambda: own_ref[...].reshape(rows, outer * LANES), other_measured],
        tables, angles_total,
    )
    for a in range(angles):
        for q in range(outer):
            back_ref[pl.ds(a * outer + q, slices, piece), :] = result[a][q]

    parity = lax.rem(ang, 2)
    mine = pl.ds(parity * chunk + (ang // 2) * piece, piece)

    def send_back(step, carry):
        there = lax.rem(ang + step, groups)
        pltpu.make_async_remote_copy(
            src_ref=back_ref.at[pl.ds(there * piece, piece)], dst_ref=out_ref.at[mine],
            send_sem=back_send, recv_sem=back_recv.at[parity],
            device_id=(there, dist), device_id_type=mesh_ids,
        ).start()
        return carry

    lax.fori_loop(1, groups, send_back, 0)
    pltpu.make_async_copy(
        back_ref.at[pl.ds(ang * piece, piece)], out_ref.at[mine], back_recv.at[parity]
    ).start()
    passes = []
    for c in range(2):
        part = out_ref.at[pl.ds(c * chunk, chunk)]
        pltpu.make_async_copy(part, part, back_recv.at[c]).wait()
        passes.append(pltpu.make_async_remote_copy(
            src_ref=part, dst_ref=out_ref.at[pl.ds((2 + c) * chunk, chunk)],
            send_sem=pass_send.at[c], recv_sem=pass_recv.at[c],
            device_id=partner, device_id_type=mesh_ids,
        ))
        passes[c].start()

    def stack_spread(rel):
        for q in range(outer):
            parts = [
                out_ref[pl.ds(rel * 2 * chunk + a * outer + q, groups, piece), :]
                for a in range(angles)
            ]
            high, low = halves(jnp.concatenate(parts, axis=0))
            count = angles * groups
            for n, value in enumerate((high, high, low)):
                first = n * angles_total + rel * count
                spread_ref[first : first + count, q * LANES : (q + 1) * LANES] = value

    stack_spread(0)
    for copy in passes:
        copy.wait()
    stack_spread(1)
    for ref, sem in ((keep_ref, send_sem), (back_ref, back_send)):
        sent = ref.at[pl.ds(0, (groups - 1) * piece)]
        pltpu.make_async_copy(sent, sent, sem).wait()
    stack_copy.wait()


def fused_call(slopes, fresnel, volume, weights, measured):
    group, slices, width = measured.shape
    angles, outer = group // 2, width // LANES
    angles_total, rows_own = weights.shape[0], volume.shape[0]
    groups = angles_total // group
    depth = -(-3 * angles_total // 256) * 256
    piece = angles * outer
    tables = column_tables(width) + row_tables(slices, angles)
    smem = pl.BlockSpec(memory_space=pltpu.SMEM)
    vmem = pl.BlockSpec(memory_space=pltpu.VMEM)
    hbm = pl.BlockSpec(memory_space=pl.ANY)
    f32 = jnp.float32
    dma = pltpu.SemaphoreType.DMA
    return pl.pallas_call(
        partial(fused_kernel, (angles, slices, outer, angles_total, rows_own, groups)),
        out_shape=(
            jax.ShapeDtypeStruct((depth, width), jnp.bfloat16),
            jax.ShapeDtypeStruct((rows_own, depth), jnp.bfloat16),
        ),
        in_specs=[smem, smem] + [hbm] * 8,
        out_specs=(vmem, hbm),
        scratch_shapes=[
            pltpu.VMEM((rows_own // LANES * angles_total, LANES), f32),
            *[pltpu.VMEM(t.shape, t.dtype) for t in tables],
            pltpu.VMEM((2 * groups * piece, LANES), f32),
            pltpu.VMEM((rows_own, depth), jnp.bfloat16),
            pltpu.VMEM((rows_own, width), f32),
            pltpu.VMEM((angles, slices, width), f32),
            pltpu.VMEM((angles, slices, width), f32),
            pltpu.VMEM((8, LANES), f32),
            pltpu.VMEM((8, LANES), f32),
            *[pltpu.VMEM((groups * piece, LANES), f32) for _ in range(3)],
            *[pltpu.VMEM((slices * piece, LANES), f32) for _ in range(2)],
            dma((9,)), *[dma((2,)) for _ in range(4)], dma, dma,
            dma, *[dma((2,)) for _ in range(3)], dma((rows_own // LANES,)),
        ],
        compiler_params=pltpu.CompilerParams(
            vmem_limit_bytes=58 * 2**20, collective_id=0, has_side_effects=True
        ),
    )(slopes, fresnel, volume, weights, measured, *[jnp.asarray(t) for t in tables])


def shards(volume, row_weights, angle_slope, shear_index, shear_weight, fresnel, measured):
    spread, weights = fused_call(angle_slope, fresnel, volume[0], row_weights, measured[0])
    return jnp.einsum("yk,kx->yx", weights, spread, preferred_element_type=jnp.float32)[None]


def solution(mesh):
    placed = (P("ang", "dist", None), P(), P(), P(), P(), P("dist"), P("dist", "ang", None, None))
    return jax.shard_map(
        shards, mesh=mesh, in_specs=placed, out_specs=P("ang", "dist", None), check_vma=False
    )
```

```python
from functools import partial
import math

import numpy as np
import jax
import jax.numpy as jnp
from jax import lax
from jax.experimental import pallas as pl
from jax.experimental.pallas import tpu as pltpu
from jax.sharding import PartitionSpec as P

ABSORB = 0.1
HIGHEST = lax.Precision.HIGHEST
LANES = 128


def dot(a, b):
    return lax.dot_general(
        a, b, (((1,), (0,)), ((), ())), precision=HIGHEST, preferred_element_type=jnp.float32
    )


def dot_narrow(a, b):
    return lax.dot_general(a, b, (((1,), (0,)), ((), ())), preferred_element_type=jnp.float32)


def halves(a):
    high = a.astype(jnp.bfloat16)
    return high, (a - high.astype(jnp.float32)).astype(jnp.bfloat16)


def dot_left(a, high, low):
    rows = a.shape[0]
    a_high, a_low = halves(a)
    both = dot_narrow(jnp.concatenate([a_high, a_low], axis=0), high)
    return both[:rows] + both[rows:] + dot_narrow(a_high, low)


def dot_right(table, table_high, b):
    rows = table_high.shape[0]
    b_high, b_low = halves(b)
    both = dot_narrow(table, b_high)
    return both[:rows] + both[rows:] + dot_narrow(table_high, b_low)


def signed_freq(counter, length):
    return np.where(counter <= (length - 1) // 2, counter, counter - length) / length


def column_tables(width):
    outer = width // LANES
    p = np.arange(LANES)
    k = np.arange(outer)
    ang = 2 * np.pi * (p[:, None] * p[None, :] % LANES) / LANES
    c, s = np.cos(ang), np.sin(ang)
    forward = np.block([[c, -s], [s, c]])
    high = forward.astype(jnp.bfloat16)
    low = (forward - high.astype(np.float64)).astype(jnp.bfloat16)
    mixed = 2 * np.pi * (k[:, None] * p[None, :] % width) / width
    freq2 = signed_freq(k[:, None] + outer * p[None, :], width) ** 2
    small = np.stack([np.cos(mixed), np.sin(mixed), freq2])
    return np.stack([high, low]), small.astype(np.float32)


def row_tables(slices, angles):
    z = np.arange(slices)
    ang = 2 * np.pi * (z[:, None] * z[None, :] % slices) / slices
    trig = np.stack([np.cos(ang), np.sin(ang)])
    rows = 2 * angles * slices
    left_r = np.zeros((2, angles, slices, 2, angles, 2, slices))
    left_i = np.zeros_like(left_r)
    right = np.zeros((2, angles, 2, slices, 2, angles, slices))
    for c in range(2):
        for a in range(angles):
            for t in range(2):
                left_r[c, a, :, c, a, t, :] = trig[t]
                left_i[c, a, :, 1 - c, a, t, :] = trig[t] * (-1.0 if c == 0 else 1.0)
                right[c, a, t, :, c, a, :] = trig[t] / slices
    freq2 = np.broadcast_to(signed_freq(z, slices) ** 2, (2, angles, 2, slices)).reshape(1, -1)
    left = np.stack([left_r.reshape(rows, -1), left_i.reshape(rows, -1)])
    return left.astype(np.float32), right.reshape(-1, rows).astype(np.float32), freq2.astype(np.float32)


def fft_list(parts, sign):
    n = len(parts)
    if n == 1:
        return parts
    even = fft_list(parts[0::2], sign)
    odd = fft_list(parts[1::2], sign)
    low, high = [], []
    for k in range(n // 2):
        (er, ei), (br, bi) = even[k], odd[k]
        if k == 0:
            tr, ti = br, bi
        elif 4 * k == n:
            tr, ti = (-bi, br) if sign > 0 else (bi, -br)
        else:
            wr = math.cos(2 * math.pi * k / n)
            wi = sign * math.sin(2 * math.pi * k / n)
            tr, ti = br * wr - bi * wi, br * wi + bi * wr
        low.append((er + tr, ei + ti))
        high.append((er - tr, ei - ti))
    return low + high


def columns_forward(parts, table, mix_cos, mix_sin):
    parts = fft_list(parts, -1)
    rows = []
    for k, (re, im) in enumerate(parts):
        c, s = mix_cos[k : k + 1], mix_sin[k : k + 1]
        rows.append(jnp.concatenate([re * c + im * s, im * c - re * s], axis=1))
    return dot_left(jnp.concatenate(rows, axis=0), *table)


def columns_inverse(spectrum, table, mix_cos, mix_sin):
    outer = mix_cos.shape[0]
    count = spectrum.shape[0] // outer
    result = dot_left(spectrum, *table)
    parts = []
    for k in range(outer):
        im = result[k * count : (k + 1) * count, :LANES]
        re = result[k * count : (k + 1) * count, LANES:]
        c, s = mix_cos[k : k + 1], mix_sin[k : k + 1]
        parts.append((re * c - im * s, im * c + re * s))
    return fft_list(parts, 1)


def tile_pairs(outer):
    pairs = []
    half = outer // 2
    for block in range(outer):
        first = LANES * (block - half)
        ends = [first, first + LANES - 1]
        low = min(min(math.floor(u * 0.5), math.floor(u * 4095 / 4096)) for u in ends)
        high = max(max(math.floor(u * 0.5), math.floor(u * 4095 / 4096)) for u in ends) + 1
        for tile in range(low // LANES + half, high // LANES + half + 1):
            if 0 <= tile < outer:
                pairs.append((block, tile))
    return pairs


def lane_take(values, index):
    return jnp.take_along_axis(values, index, axis=1, mode="promise_in_bounds")


def band_forward(tiles, step):
    outer, count = len(tiles), tiles[0].shape[0]
    lane = lax.broadcasted_iota(jnp.int32, (1, LANES), 1).astype(jnp.float32)
    center = float(outer // 2 * LANES)
    result = [None] * outer
    for block in range(outer):
        place = step * (lane + (LANES * block - center)) * (1.0 / 4096.0)
        lower = jnp.floor(place)
        weight = place - lower
        for shift, coef in ((0.0, 1.0 - weight), (1.0, weight)):
            source = lower + (center + shift)
            tile_of = jnp.floor(source * (1.0 / LANES))
            inside = (source - LANES * tile_of).astype(jnp.int32)
            index = jnp.broadcast_to(inside, (count, LANES))
            for pair_block, tile in tile_pairs(outer):
                if pair_block != block:
                    continue
                term = jnp.where(tile_of == float(tile), coef, 0.0) * lane_take(tiles[tile], index)
                result[block] = term if result[block] is None else result[block] + term
    return result


def band_backward(blocks, step):
    outer, count = len(blocks), blocks[0].shape[0]
    lane = lax.broadcasted_iota(jnp.int32, (1, LANES), 1).astype(jnp.float32)
    center = float(outer // 2 * LANES)
    result = [None] * outer
    for tile in range(outer):
        target = (lane + (LANES * tile - center)) * 4096.0
        first = jnp.floor(target / step)
        for shift in (-1.0, 0.0, 1.0, 2.0):
            source = first + shift
            coef = jnp.maximum(4096.0 - jnp.abs(step * source - target), 0.0) * (1.0 / 4096.0)
            place = source + center
            block_of = jnp.floor(place * (1.0 / LANES))
            inside = (place - LANES * block_of).astype(jnp.int32)
            index = jnp.broadcast_to(inside, (count, LANES))
            for block, pair_tile in tile_pairs(outer):
                if pair_tile != tile:
                    continue
                term = jnp.where(block_of == float(block), coef, 0.0) * lane_take(blocks[block], index)
                result[tile] = term if result[tile] is None else result[tile] + term
    return result


def image_step(ray_tiles, slopes, fresnels, measured, tables, angles_total):
    forward, small, left, right, row_freq2 = tables
    angles, outer = len(ray_tiles), len(ray_tiles[0])
    slices = ray_tiles[0][0].shape[0]
    rows = angles * slices
    width = outer * LANES
    mix_cos, mix_sin, col_freq2 = small
    scales, steps = [], []
    for slope in slopes:
        value = slope.astype(jnp.float32)
        steps.append(value + 3072.0)
        tangent = jnp.full((1, LANES), value) * (1.0 / 512.0)
        scales.append(jnp.sqrt(1.0 + tangent * tangent))
    images = [band_forward(ray_tiles[a], steps[a]) for a in range(angles)]
    waves = []
    for q in range(outer):
        image = jnp.concatenate([images[a][q] * scales[a] for a in range(angles)], axis=0)
        fade = jnp.exp(-ABSORB * image)
        waves.append((fade * jnp.cos(image), fade * jnp.sin(image)))
    spectrum = columns_forward(waves, forward, mix_cos, mix_sin)
    spec_re = [spectrum[k * rows : (k + 1) * rows, :LANES] for k in range(outer)]
    spec_im = [spectrum[k * rows : (k + 1) * rows, LANES:] for k in range(outer)]
    total = [None] * outer
    for d in range(len(fresnels)):
        phase = (math.pi * fresnels[d]) * col_freq2
        col_cos, col_sin = jnp.cos(phase), jnp.sin(phase)
        row_phase = (math.pi * fresnels[d]) * row_freq2
        left_cos, left_sin = left[0] * jnp.cos(row_phase), left[1] * jnp.sin(row_phase)
        mix = jnp.concatenate(halves(dot(left_cos - left_sin, right)), axis=0)
        mix_back = jnp.concatenate(halves(dot(left_cos + left_sin, right)), axis=0)
        scaled = []
        for k in range(outer):
            c, s = col_cos[k : k + 1], col_sin[k : k + 1]
            re, im = spec_re[k], spec_im[k]
            scaled.append(jnp.concatenate([im * c - re * s, re * c + im * s], axis=1))
        parts = columns_inverse(jnp.concatenate(scaled, axis=0), forward, mix_cos, mix_sin)
        stacked = jnp.concatenate([jnp.concatenate(part, axis=0) for part in parts], axis=1)
        field = dot_right(mix, mix[: 2 * rows], stacked * (1.0 / width))
        re, im = field[:rows], field[rows:]
        slope_of = (re * re + im * im - measured[d]()) * (4.0 / angles_total)
        back = dot_right(mix_back, mix_back[: 2 * rows], jnp.concatenate([slope_of * re, slope_of * im], axis=0))
        pieces = [
            (back[:rows, q * LANES : (q + 1) * LANES], back[rows:, q * LANES : (q + 1) * LANES])
            for q in range(outer)
        ]
        adjoint = columns_forward(pieces, forward, mix_cos, mix_sin)
        for k in range(outer):
            c, s = col_cos[k : k + 1], col_sin[k : k + 1]
            re = adjoint[k * rows : (k + 1) * rows, :LANES]
            im = adjoint[k * rows : (k + 1) * rows, LANES:]
            term = jnp.concatenate([im * c + re * s, re * c - im * s], axis=1)
            total[k] = term if total[k] is None else total[k] + term
    parts = columns_inverse(jnp.concatenate(total, axis=0), forward, mix_cos, mix_sin)
    grads = []
    for q in range(outer):
        (re, im), (wave_re, wave_im) = parts[q], waves[q]
        re, im = re * (1.0 / width), im * (1.0 / width)
        grads.append(re * (-ABSORB * wave_re - wave_im) + im * (wave_re - ABSORB * wave_im))
    result = []
    for a in range(angles):
        own = [g[a * slices : (a + 1) * slices] * scales[a] for g in grads]
        result.append(band_backward(own, steps[a]))
    return result


def fused_kernel(
    sizes, slope_ref, fresnel_ref, volume_hbm, weight_hbm, measured_hbm,
    forward_hbm, small_hbm, left_hbm, right_hbm, freq_hbm, spread_ref, stack_ref,
    weight_ref, forward_ref, small_ref, left_ref, right_ref, freq_ref, out_ref,
    volume_ref, own_ref, other_ref, fresnel_out, fresnel_in, send_ref, recv_ref, back_ref,
    local_sem, swap_send, swap_recv, send_sem, recv_sem, back_send, back_recv,
):
    angles, slices, outer, angles_total, rows_own, devices = sizes
    ang, dist = lax.axis_index("ang"), lax.axis_index("dist")
    me = ang * 2 + dist
    piece = angles * outer
    rows = angles * slices
    barrier = pltpu.get_barrier_semaphore()

    def place_of(step):
        there = lax.rem(me + step, devices)
        return there, (there // 2, lax.rem(there, 2))

    weight_copy = pltpu.make_async_copy(
        weight_hbm.at[:, pl.ds(pl.multiple_of(dist * rows_own, LANES), rows_own)],
        weight_ref, local_sem.at[2],
    )
    weight_copy.start()
    volume_copy = pltpu.make_async_copy(volume_hbm, volume_ref, local_sem.at[0])
    volume_copy.start()
    own_copy = pltpu.make_async_copy(
        measured_hbm.at[pl.ds(dist * angles, angles)], own_ref, local_sem.at[1]
    )
    own_copy.start()
    table_copies = []
    for n, (source, target) in enumerate((
        (forward_hbm, forward_ref), (small_hbm, small_ref), (left_hbm, left_ref),
        (right_hbm, right_ref), (freq_hbm, freq_ref),
    )):
        table_copies.append(pltpu.make_async_copy(source, target, local_sem.at[3 + n]))
        table_copies[n].start()

    def greet(step, carry):
        pl.semaphore_signal(
            barrier, inc=1, device_id=place_of(step)[1], device_id_type=pl.DeviceIdType.MESH
        )
        return carry

    lax.fori_loop(1, devices, greet, 0)
    fresnel_out[...] = jnp.full(fresnel_out.shape, fresnel_ref[0])
    weight_copy.wait()
    weight_high, weight_low = halves(weight_ref[...])
    weights = jnp.concatenate([weight_high, weight_low], axis=0)
    stack_ref[...] = jnp.concatenate([weight_high, weight_low, weight_high], axis=0)
    volume_copy.wait()
    for q in range(0, outer, 2):
        high, low = halves(volume_ref[:, q * LANES : (q + 2) * LANES])
        both = dot_narrow(weights, high) + dot_narrow(weights, low)
        total = both[:angles_total] + both[angles_total:]
        send_ref[pl.ds(q, angles_total, outer), :] = total[:, :LANES]
        send_ref[pl.ds(q + 1, angles_total, outer), :] = total[:, LANES:]
    pl.semaphore_wait(barrier, devices - 1)

    def send(step, carry):
        there, target = place_of(step)
        pltpu.make_async_remote_copy(
            src_ref=send_ref.at[pl.ds(there * piece, piece)],
            dst_ref=recv_ref.at[pl.ds(me * piece, piece)],
            send_sem=send_sem, recv_sem=recv_sem,
            device_id=target, device_id_type=pl.DeviceIdType.MESH,
        ).start()
        return carry

    swaps = []
    for n, (source, target) in enumerate((
        (fresnel_out, fresnel_in),
        (measured_hbm.at[pl.ds((1 - dist) * angles, angles)], other_ref),
    )):
        swaps.append(pltpu.make_async_remote_copy(
            src_ref=source, dst_ref=target, send_sem=swap_send.at[n], recv_sem=swap_recv.at[n],
            device_id=(ang, 1 - dist), device_id_type=pl.DeviceIdType.MESH,
        ))
    swaps[0].start()
    lax.fori_loop(1, devices, send, 0)
    pltpu.make_async_copy(
        send_ref.at[pl.ds(me * piece, piece)], recv_ref.at[pl.ds(me * piece, piece)], recv_sem
    ).start()
    swaps[1].start()
    own_copy.wait()
    for copy in table_copies:
        copy.wait()
    swaps[0].wait()
    fresnels = [fresnel_out[0:1, 0:1], fresnel_in[0:1, 0:1]]
    shift = devices - 1
    pltpu.make_async_copy(recv_ref, recv_ref, recv_sem).wait()
    part = send_ref.at[pl.ds(0, shift * piece)]
    pltpu.make_async_copy(part, part, send_sem).wait()
    stride = 2 * piece
    rays = []
    for a in range(angles):
        rays.append([
            recv_ref[pl.ds(a * outer + q, slices, stride), :]
            + recv_ref[pl.ds((angles + a) * outer + q, slices, stride), :]
            for q in range(outer)
        ])
    tables = (
        (forward_ref[0], forward_ref[1]), (small_ref[0], small_ref[1], small_ref[2]),
        (left_ref[0], left_ref[1]), right_ref[...], freq_ref[...],
    )
    def other_measured():
        swaps[1].wait()
        return other_ref[...].reshape(rows, outer * LANES)

    result = image_step(
        rays, [slope_ref[me * angles + a] for a in range(angles)], fresnels,
        [lambda: own_ref[...].reshape(rows, outer * LANES), other_measured],
        tables, angles_total,
    )
    for a in range(angles):
        for q in range(outer):
            back_ref[pl.ds(a * outer + q, slices, piece), :] = result[a][q]

    def send_back(step, carry):
        there, target = place_of(step)
        pltpu.make_async_remote_copy(
            src_ref=back_ref.at[pl.ds((there // 2) * piece, piece)],
            dst_ref=out_ref.at[pl.ds(me * piece, piece)],
            send_sem=back_send, recv_sem=back_recv,
            device_id=target, device_id_type=pl.DeviceIdType.MESH,
        ).start()
        return carry

    lax.fori_loop(1, devices, send_back, 0)
    pltpu.make_async_copy(
        back_ref.at[pl.ds(ang * piece, piece)], out_ref.at[pl.ds(me * piece, piece)], back_recv
    ).start()
    pltpu.make_async_copy(out_ref, out_ref, back_recv).wait()
    sent = out_ref.at[pl.ds(0, shift * piece)]
    pltpu.make_async_copy(sent, sent, back_send).wait()
    for q in range(outer):
        high, low = halves(out_ref[pl.ds(q, angles_total, outer), :])
        spread_ref[:, q * LANES : (q + 1) * LANES] = jnp.concatenate([high, high, low], axis=0)


def fused_call(slopes, fresnel, volume, weights, measured):
    group, slices, width = measured.shape
    angles, outer = group // 2, width // LANES
    angles_total, rows_own = weights.shape[0], volume.shape[0]
    devices = angles_total // angles
    piece = angles * outer
    tables = column_tables(width) + row_tables(slices, angles)
    smem = pl.BlockSpec(memory_space=pltpu.SMEM)
    vmem = pl.BlockSpec(memory_space=pltpu.VMEM)
    hbm = pl.BlockSpec(memory_space=pl.ANY)
    f32 = jnp.float32
    dma = pltpu.SemaphoreType.DMA
    return pl.pallas_call(
        partial(fused_kernel, (angles, slices, outer, angles_total, rows_own, devices)),
        out_shape=(
            jax.ShapeDtypeStruct((3 * angles_total, width), jnp.bfloat16),
            jax.ShapeDtypeStruct((3 * angles_total, rows_own), jnp.bfloat16),
        ),
        in_specs=[smem, smem] + [hbm] * 8,
        out_specs=(vmem, vmem),
        scratch_shapes=[
            pltpu.VMEM((angles_total, rows_own), f32),
            *[pltpu.VMEM(t.shape, t.dtype) for t in tables],
            pltpu.VMEM((devices * piece, LANES), f32),
            pltpu.VMEM((rows_own, width), f32),
            pltpu.VMEM((angles, slices, width), f32),
            pltpu.VMEM((angles, slices, width), f32),
            pltpu.VMEM((8, LANES), f32),
            pltpu.VMEM((8, LANES), f32),
            pltpu.VMEM((devices * piece, LANES), f32),
            pltpu.VMEM((devices * piece, LANES), f32),
            pltpu.VMEM((slices * piece, LANES), f32),
            dma((8,)), dma((2,)), dma((2,)), dma, dma, dma, dma,
        ],
        compiler_params=pltpu.CompilerParams(
            vmem_limit_bytes=58 * 2**20, collective_id=0, has_side_effects=True
        ),
    )(slopes, fresnel, volume, weights, measured, *[jnp.asarray(t) for t in tables])


def shards(volume, row_weights, angle_slope, shear_index, shear_weight, fresnel, measured):
    spread, weights = fused_call(angle_slope, fresnel, volume[0], row_weights, measured[0])
    return jnp.einsum("ky,kx->yx", weights, spread, preferred_element_type=jnp.float32)[None]


def solution(mesh):
    placed = (P("ang", "dist", None), P(), P(), P(), P(), P("dist"), P("dist", "ang", None, None))
    return jax.shard_map(
        shards, mesh=mesh, in_specs=placed, out_specs=P("ang", "dist", None), check_vma=False
    )
```
